32 devices in a mesh: rep: 2 (over x), fsdp: 16 (over z, y, core).
Axes of the slice: x: 2, y: 2, z: 4, core: 2. Of those that a mesh axis runs over, the one named last changes fastest.
Arguments:
- tokens: bfloat16 [512, 4096], P(('rep', 'fsdp')), may hold values from -6 to 6
- upstream: bfloat16 [512, 14336], P(('rep', 'fsdp')), may hold values from -6 to 6
- blocks: bfloat16 [224, 16, 128, 128], P('fsdp'), may hold values from -0.125 to 0.125
- keep_mask: int32 [32, 112], replicated, may hold values from 0 to 1, as said below
- panel_owner: int32 [112], replicated, may hold values from 0 to 15, as said below
Outputs:
- activation: bfloat16 [512, 14336], P(('rep', 'fsdp'))
- input_grad: bfloat16 [512, 4096], P(('rep', 'fsdp'))
- block_grad: bfloat16 [224, 16, 128, 128], P('fsdp')
The draws below stay inside these ranges and needn't reach their ends.
Inputs may be any that keep to these rules, and one draw needn't show every extreme that they name: `keep_mask`: every column panel keeps exactly 16 of its 32 blocks. `panel_owner`: non-decreasing over the panels; a shard owns at most 14 panels, some shard owns exactly 14, and some shard owns none.
All inputs are finite; a program needn't handle non-finite values.
Results may differ from the reference program's by a relative error of at most 0.005.
Values may be sent and summed in bfloat16 or wider, within the bound.
A program may use at most 128 MiB of HBM per device.

```python
import math
import jax
import jax.numpy as jnp
from jax import lax

D = 4096
FF = 14336
BS = 128
RB = 32
CB = 112
KEEP = 16
PMAX = 14
TOKENS = 512
N_FSDP = 16


def draw_keep_mask(key, part):
    key = jax.random.fold_in(key, 11)
    column_keys = jax.random.split(key, CB)

    def column(column_key):
        shuffled = jax.random.permutation(column_key, RB)
        return (shuffled < KEEP).astype(jnp.int32)
    return jnp.transpose(jax.vmap(column)(column_keys))


def draw_panel_owner(key, part):
    key = jax.random.fold_in(key, 23)
    order_key, share_key, forced_key, flip_key, move_key = jax.random.split(key, 5)
    pair_count = N_FSDP // 2
    share_low = jax.random.randint(share_key, (pair_count,), 0, PMAX + 1).astype(jnp.int32)
    forced = jax.random.randint(forced_key, (), 0, pair_count).astype(jnp.int32)
    pair_ids = jnp.arange(pair_count, dtype=jnp.int32)
    share_low = jnp.where(pair_ids == forced, PMAX, share_low).astype(jnp.int32)
    flip_bits = jax.random.randint(flip_key, (pair_count,), 0, 2)
    first_count = jnp.where(flip_bits == 1, share_low, PMAX - share_low).astype(jnp.int32)
    second_count = (PMAX - first_count).astype(jnp.int32)
    paired = jnp.stack([first_count, second_count], axis=1).reshape(-1).astype(jnp.int32)
    order = jax.random.permutation(order_key, N_FSDP).astype(jnp.int32)
    counts = jnp.zeros((N_FSDP,), jnp.int32).at[order].set(paired)
    guard_one = order[2 * forced]
    guard_two = order[2 * forced + 1]

    def move_unit(step, counts_now):
        step_key = jax.random.fold_in(move_key, step)
        picks = jax.random.randint(step_key, (2,), 0, N_FSDP).astype(jnp.int32)
        donor = picks[0]
        taker = picks[1]
        allowed = (donor != taker) & (counts_now[donor] > 0) & (counts_now[taker] < PMAX)
        allowed = allowed & (donor != guard_one) & (donor != guard_two)
        allowed = allowed & (taker != guard_one) & (taker != guard_two)
        delta = allowed.astype(jnp.int32)
        counts_now = counts_now.at[donor].add(-delta)
        return counts_now.at[taker].add(delta)
    counts = lax.fori_loop(0, 4 * N_FSDP, move_unit, counts)
    range_ends = jnp.cumsum(counts).astype(jnp.int32)
    panels = jnp.arange(CB, dtype=jnp.int32)
    return jnp.sum((range_ends[None, :] <= panels[:, None]).astype(jnp.int32), axis=1).astype(jnp.int32)


def block_scale(stream_key, shape, shards, least, largest):
    loudness, own = 1.0, jax.random.fold_in(stream_key, 6)
    for axis_at, parts in shards:
        steps = jnp.exp(jax.random.uniform(jax.random.fold_in(own, axis_at), (parts,), jnp.float32, least / len(shards), largest / len(shards)))
        loudness = loudness * jnp.repeat(steps, shape[axis_at] // parts).reshape([-1 if axis == axis_at else 1 for axis in range(len(shape))])
    return loudness


def scatter_about(stream_key, dims, width, bound, shards=(), held_as=jnp.bfloat16):
    drawn = jax.random.normal(stream_key, dims, jnp.float32) * width
    if len(shards) > 0:
        drawn = block_scale(stream_key, dims, shards, -0.22, 0.18) * drawn
    return jnp.clip(drawn, min=-bound, max=bound).astype(held_as)


def setup_inputs(seed: int = 0) -> dict:
    key_list = jax.random.split(jax.random.key(seed), 6)
    return {
        "tokens": scatter_about(key_list[0], (TOKENS, D), 1.0, 6.0, ((0, 32),)),
        "upstream": scatter_about(key_list[1], (TOKENS, FF), 1.0, 6.0, ((0, 32),)),
        "blocks": scatter_about(key_list[2], (N_FSDP * PMAX, KEEP, BS, BS), (KEEP * BS) ** -0.5, 0.125, ((0, 16),)),
        "keep_mask": draw_keep_mask(jax.random.fold_in(key_list[5], 71), 0),
        "panel_owner": draw_panel_owner(jax.random.fold_in(key_list[5], 71), 0),
    }


def layout_tables(keep_mask, panel_owner):
    shard_ids = jnp.arange(N_FSDP, dtype=jnp.int32)
    member = (panel_owner[:, None] == shard_ids[None, :]).astype(jnp.int32)
    counts = lax.optimization_barrier(jnp.sum(member, axis=0)).astype(jnp.int32)
    first_panel = (jnp.cumsum(counts) - counts).astype(jnp.int32)
    slot_ids = jnp.arange(PMAX, dtype=jnp.int32)
    panel_table = jnp.clip(first_panel[:, None] + slot_ids[None, :], 0, CB - 1).astype(jnp.int32)
    slot_live = slot_ids[None, :] < counts[:, None]
    running = jnp.cumsum(keep_mask, axis=0).astype(jnp.int32)
    pick_ids = jnp.arange(KEEP, dtype=jnp.int32)
    kept_rows = lax.optimization_barrier(jnp.sum((running[:, :, None] <= pick_ids[None, None, :]).astype(jnp.int32), axis=0)).astype(jnp.int32)
    panel_ids = jnp.arange(CB, dtype=jnp.int32)
    panel_slot = (panel_owner * PMAX + panel_ids - first_panel[panel_owner]).astype(jnp.int32)
    return (panel_table, slot_live, running, kept_rows, panel_slot)

def reference(tokens, upstream, blocks, keep_mask, panel_owner):
    panel_table, slot_live, running, kept_rows, panel_slot = layout_tables(keep_mask, panel_owner)
    rank = jnp.clip(running - 1, 0, KEEP - 1).astype(jnp.int32)
    placed = blocks[panel_slot[None, :], rank]
    placed = jnp.where(keep_mask[:, :, None, None] == 1, placed, jnp.zeros((), blocks.dtype))
    weight = jnp.transpose(placed, (0, 2, 1, 3)).reshape(D, FF)
    preact = jnp.dot(tokens, weight, preferred_element_type=jnp.float32)
    activation = jax.nn.silu(preact).astype(jnp.bfloat16)
    sigmoid_z = jax.nn.sigmoid(preact)
    slope = sigmoid_z * (1.0 + preact * (1.0 - sigmoid_z))
    dpre = (upstream.astype(jnp.float32) * slope).astype(jnp.bfloat16)
    dpre3 = dpre.reshape(TOKENS, CB, BS)
    weight3 = weight.reshape(D, CB, BS)

    def owner_term(accum_rows, owner_id):
        columns = panel_table[owner_id]
        is_live = slot_live[owner_id]
        picked = jnp.take(dpre3, columns, axis=1)
        picked = jnp.where(is_live[None, :, None], picked, jnp.zeros((), dpre.dtype))
        weights_k = jnp.take(weight3, columns, axis=1)
        term = lax.dot_general(picked.reshape(TOKENS, PMAX * BS), weights_k.reshape(D, PMAX * BS), (((1,), (1,)), ((), ())), preferred_element_type=jnp.float32)
        return (accum_rows + term, None)
    summed, ignored = lax.scan(owner_term, jnp.zeros((TOKENS, D), jnp.float32), jnp.arange(N_FSDP, dtype=jnp.int32))
    input_grad = summed.astype(jnp.bfloat16)
    full_grad = lax.dot_general(tokens, dpre, (((0,), (0,)), ((), ())), preferred_element_type=jnp.float32)
    full4 = full_grad.reshape(RB, BS, CB, BS)
    flat_panels = panel_table.reshape(-1)
    row_ids = kept_rows[flat_panels]
    gathered = full4[row_ids, :, flat_panels[:, None], :]
    scaled = gathered * (1.0 / math.sqrt(TOKENS))
    live_flat = slot_live.reshape(-1)
    block_grad = jnp.where(live_flat[:, None, None, None], scaled, 0.0).astype(jnp.bfloat16)
    return (activation, input_grad, block_grad)
```

```python
import functools
import math

import jax
import jax.numpy as jnp
from jax import lax
from jax.experimental import pallas as pl
from jax.experimental.pallas import tpu as pltpu
from jax.sharding import PartitionSpec as P

BF16 = jnp.bfloat16
F32 = jnp.float32
MESH = pl.DeviceIdType.MESH
VMEM_LIMIT = 60 * 1024 * 1024
NZ, NY, NC = 4, 2, 2
NF = NZ * NY * NC


def per_device_general(tokens, upstream, blocks, keep_mask, panel_owner):
    shard_count = lax.axis_size("fsdp")
    own_index = lax.axis_index("fsdp")
    tok_dev = tokens.shape[0]
    model_width = tokens.shape[1]
    slot_count = blocks.shape[0]
    keep_count = blocks.shape[1]
    block_size = blocks.shape[3]
    row_blocks = keep_mask.shape[0]
    panel_count = panel_owner.shape[0]
    group_rows = tok_dev * shard_count
    rep_count = lax.axis_size("rep")
    shard_ids = jnp.arange(shard_count, dtype=jnp.int32)
    member = (panel_owner[:, None] == shard_ids[None, :]).astype(jnp.int32)
    counts = jnp.sum(member, axis=0)
    first_panel = jnp.cumsum(counts) - counts
    slot_ids = jnp.arange(slot_count, dtype=jnp.int32)
    panel_table = jnp.clip(first_panel[:, None] + slot_ids[None, :], 0, panel_count - 1)
    is_mine = shard_ids == own_index
    own_first = jnp.sum(jnp.where(is_mine, first_panel, 0))
    own_count = jnp.sum(jnp.where(is_mine, counts, 0))
    own_live = slot_ids < own_count
    own_panels = jnp.clip(own_first + slot_ids, 0, panel_count - 1)
    panel_ids = jnp.arange(panel_count, dtype=jnp.int32)
    panel_pick = (panel_ids[None, :] == own_panels[:, None]).astype(jnp.int32)
    running = jnp.cumsum(keep_mask, axis=0)
    own_running = jnp.sum(panel_pick[:, None, :] * running[None, :, :], axis=2)
    pick_ids = jnp.arange(keep_count, dtype=jnp.int32)
    own_rows = jnp.sum(
        (own_running[:, :, None] <= pick_ids[None, None, :]).astype(jnp.int32), axis=1
    )
    upstream_panels = jnp.transpose(upstream.reshape(tok_dev, panel_count, block_size), (1, 0, 2))
    outgoing = jnp.take(upstream_panels, panel_table.reshape(-1), axis=0)
    incoming = lax.all_to_all(outgoing, "fsdp", split_axis=0, concat_axis=1, tiled=True)
    group_tokens = lax.all_gather(tokens, "fsdp", axis=0, tiled=True)
    all_tokens = lax.all_gather(group_tokens, "rep", axis=0, tiled=True)
    token_blocks = jnp.transpose(all_tokens).reshape(row_blocks, block_size, rep_count * group_rows)

    dense_panels = jnp.zeros((slot_count, row_blocks, block_size, block_size), blocks.dtype)
    dense_panels = dense_panels.at[slot_ids[:, None], own_rows].set(blocks)
    dense = dense_panels.reshape(slot_count, model_width, block_size)
    preact = lax.dot_general(
        group_tokens, dense, (((1,), (1,)), ((), ())), preferred_element_type=jnp.float32
    )
    sigmoid_z = jax.nn.sigmoid(preact)
    activations = (preact * sigmoid_z).astype(jnp.bfloat16)
    slope = sigmoid_z * (1.0 + preact * (1.0 - sigmoid_z))
    cot = jnp.transpose(incoming, (1, 0, 2)).astype(jnp.float32)
    dpre = jnp.where(own_live[None, :, None], cot * slope, 0.0).astype(jnp.bfloat16)
    dpre_all = lax.all_gather(dpre, "rep", axis=0, tiled=True)
    backward = lax.dot_general(
        dpre, dense, (((1, 2), (0, 2)), ((), ())), preferred_element_type=jnp.float32
    )
    input_grad = lax.psum_scatter(
        backward, "fsdp", scatter_dimension=0, tiled=True
    ).astype(jnp.bfloat16)
    returned = lax.all_to_all(activations, "fsdp", split_axis=0, concat_axis=1, tiled=True)
    panel_first = jnp.sum(member * first_panel[None, :], axis=1)
    panel_slot = panel_owner * slot_count + panel_ids - panel_first
    act_panels = jnp.take(returned, panel_slot, axis=1)
    activation_out = act_panels.reshape(tok_dev, panel_count * block_size)
    scale = 1.0 / math.sqrt(group_rows * rep_count)

    def panel_step(nothing, item):
        row_ids, dz = item
        chosen = jnp.take(token_blocks, row_ids, axis=0)
        grad = lax.dot_general(
            chosen, dz, (((2,), (0,)), ((), ())), preferred_element_type=jnp.float32
        )
        return nothing, (grad * scale).astype(jnp.bfloat16)

    nothing, block_grad = lax.scan(
        panel_step, jnp.zeros((), jnp.float32), (own_rows, jnp.transpose(dpre_all, (1, 0, 2)))
    )
    return (activation_out, input_grad, block_grad)


class Place:
    def __init__(self):
        self.rep = lax.axis_index("rep")
        self.me = lax.axis_index("fsdp")
        self.core = self.me % NC
        self.y = (self.me // NC) % NY
        self.z = self.me // (NC * NY)

    def at(self, z, y, core):
        return (z * NY + y) * NC + core

    def z_back(self, step):
        return (self.z + NZ - step) % NZ

    def z_ahead(self, step):
        return (self.z + step) % NZ

    def fsdp_peer(self, step):
        return (self.me + step) % NF

    def greet(self):
        barrier = pltpu.get_barrier_semaphore()
        for step in range(1, NF):
            pl.semaphore_signal(
                barrier, inc=1, device_id=(self.rep, self.fsdp_peer(step)), device_id_type=MESH
            )
        pl.semaphore_signal(barrier, inc=1, device_id=(1 - self.rep, self.me), device_id_type=MESH)
        pl.semaphore_wait(barrier, NF)


def send(src, dst, sems, slot, device):
    send_sems, recv_sems = sems
    copy = pltpu.make_async_remote_copy(
        src_ref=src,
        dst_ref=dst,
        send_sem=send_sems.at[slot],
        recv_sem=recv_sems.at[slot],
        device_id=device,
        device_id_type=MESH,
    )
    copy.start()
    return copy


def pick_kernel(table, upstream, outgoing):
    slots, bs = outgoing.shape[1], outgoing.shape[3]

    @pl.loop(0, outgoing.shape[0])
    def _(k):
        for p in range(slots):
            column = pl.multiple_of(table[k * slots + p] * bs, bs)
            outgoing[k, p] = upstream[:, pl.ds(column, bs)]


def gather_kernel(
    tokens, outgoing, all_tokens, incoming,
    z_s, z_r, y_s, y_r, x_s, x_r, d_s, d_r, c_s, c_r, u_s, u_r,
):
    place = Place()
    rep, me, z, y, core = place.rep, place.me, place.z, place.y, place.core
    y_peer = (rep, place.at(z, 1 - y, core))
    x_peer = (1 - rep, me)
    core_peer = (rep, place.at(z, y, 1 - core))
    z_sems, y_sems, x_sems = (z_s, z_r), (y_s, y_r), (x_s, x_r)
    d_sems, c_sems, u_sems = (d_s, d_r), (c_s, c_r), (u_s, u_r)

    all_tokens[rep, me] = tokens[...]
    place.greet()
    pending = []
    own = all_tokens.at[rep, me]
    z_copies = {}
    for step in range(1, NZ):
        peer = (rep, place.at(place.z_ahead(step), y, core))
        z_copies[step] = send(own, own, z_sems, step - 1, peer)
    pending += list(z_copies.values())
    y_copies, x_copies, d_copies, c_copies = [], [], [None] * NZ, []

    def spread(step):
        piece = all_tokens.at[rep, place.at(place.z_back(step), y, core)]
        x_copies.append(send(piece, piece, x_sems, step, x_peer))
        y_copies.append(send(piece, piece, y_sems, step, y_peer))
        c_copies.append(send(piece, piece, c_sems, step, core_peer))

    spread(0)

    incoming[me] = outgoing[me]
    u_copies = []
    for step in range(1, NF):
        peer = place.fsdp_peer(step)
        u_copies.append(
            send(outgoing.at[peer], incoming.at[me], u_sems, step - 1, (rep, peer))
        )
    for step in range(1, NZ):
        z_copies[step].wait_recv()
        spread(step)
    for step in range(NZ):
        f_x = place.at(place.z_back(step), y, core)
        f_y = place.at(place.z_back(step), 1 - y, core)
        x_copies[step].wait_recv()
        piece = all_tokens.at[1 - rep, f_x]
        if step % 2 == 0:
            d_copies[step] = send(piece, piece, d_sems, step, y_peer)
        c_copies.append(send(piece, piece, c_sems, NZ + step, core_peer))
        y_copies[step].wait_recv()
        piece = all_tokens.at[rep, f_y]
        if step % 2 == 1:
            d_copies[step] = send(piece, piece, d_sems, step, x_peer)
        c_copies.append(send(piece, piece, c_sems, 2 * NZ + step, core_peer))
    for step in range(NZ):
        d_copies[step].wait_recv()
        piece = all_tokens.at[1 - rep, place.at(place.z_back(step), 1 - y, core)]
        c_copies.append(send(piece, piece, c_sems, 3 * NZ + step, core_peer))
    for copy in c_copies:
        copy.wait_recv()
    for copy in u_copies:
        copy.wait_recv()
    for copy in pending + y_copies + x_copies + d_copies + c_copies + u_copies:
        copy.wait_send()


def forward_kernel(
    info, tokens, blocks, cotangent, act, dz, part, dense, dz_all
):
    pair = pl.program_id(0)
    pairs = pl.num_programs(0)
    keep, bs = blocks.shape[1], blocks.shape[2]
    rows = tokens.shape[1] * tokens.shape[2]
    width = tokens.shape[3]
    lanes = pl.ds(pl.multiple_of(pair * 2 * bs, 2 * bs), 2 * bs)
    dense[:, lanes] = jnp.zeros((width, 2 * bs), BF16)
    for side in range(2):
        side_lanes = pl.ds(pl.multiple_of(pair * 2 * bs + side * bs, bs), bs)
        for j in range(keep):
            row = info[2 + (2 * pair + side) * keep + j]
            dense[pl.ds(pl.multiple_of(row * bs, bs), bs), side_lanes] = blocks[side, j]
    preact = jnp.dot(
        tokens[0].reshape(rows, width), dense[:, lanes], preferred_element_type=F32
    )
    for side in range(2):
        zed = preact[:, side * bs:(side + 1) * bs]
        sig = jax.nn.sigmoid(zed)
        act[:, side] = (zed * sig).astype(BF16).reshape(act.shape[0], act.shape[2], bs)
        slope = sig * (1.0 + zed * (1.0 - sig))
        cot = cotangent[:, side].reshape(rows, bs).astype(F32)
        live = 2 * pair + side < info[1]
        value = jnp.where(live, cot * slope, 0.0).astype(BF16)
        dz[side] = value
        dz_all[:, pl.ds(pl.multiple_of(pair * 2 * bs + side * bs, bs), bs)] = value

    @pl.when(pair == pairs - 1)
    def _():
        chunk = 512

        @pl.loop(0, width // chunk)
        def _(n):
            span = pl.ds(pl.multiple_of(n * chunk, chunk), chunk)
            value = lax.dot_general(
                dz_all[...], dense[span, :], (((1,), (1,)), ((), ())), preferred_element_type=F32
            )
            part[:, :, span] = value.astype(BF16).reshape(part.shape[0], part.shape[1], chunk)


def scatter_kernel(
    table, dz, act, part, dz_both, act_out, grad_out,
    act_in, r1, s2, r2, s3, r3,
    x_s, x_r, a_s, a_r, s1_s, s1_r, s2_s, s2_r, s3_s, s3_r,
):
    place = Place()
    rep, me, z, y, core = place.rep, place.me, place.z, place.y, place.core
    slots = act.shape[1]
    bs = act.shape[3]
    panels = act_out.shape[1] // bs
    y_peer = (rep, place.at(z, 1 - y, core))
    core_peer = (rep, place.at(z, y, 1 - core))
    place.greet()
    sends = []
    one = []
    for turn in range(NY):
        to_y = (y + 1 + turn) % NY
        for step in range(NZ):
            to_z = place.z_ahead(step)
            one.append(send(
                part.at[place.at(to_z, to_y, 1 - core)],
                r1.at[turn * NZ + step],
                (s1_s, s1_r), turn * NZ + step, core_peer,
            ))
    x_copy = send(dz, dz_both.at[rep], (x_s, x_r), 0, (1 - rep, me))
    a_copies = []
    for step in range(1, NF):
        peer = place.fsdp_peer(step)
        a_copies.append(send(
            act.at[peer], act_in.at[pl.ds(me * slots, slots)], (a_s, a_r), step - 1, (rep, peer)
        ))
    dz_both[rep] = dz[...]
    act_in[pl.ds(me * slots, slots)] = act[me]
    two = []
    for step in range(NZ):
        one[step].wait_recv()
        f = place.at(place.z_ahead(step), 1 - y, core)
        s2[step] = (part[f].astype(F32) + r1[step].astype(F32)).astype(BF16)
        two.append(send(s2.at[step], r2.at[step], (s2_s, s2_r), step, y_peer))

    def mine(step):
        one[NZ + step].wait_recv()
        two[step].wait_recv()
        f = place.at(place.z_ahead(step), y, core)
        return part[f].astype(F32) + r1[NZ + step].astype(F32) + r2[step].astype(F32)

    three = []
    for step in range(1, NZ):
        s3[step - 1] = mine(step).astype(BF16)
        peer = (rep, place.at(place.z_ahead(step), y, core))
        three.append(send(s3.at[step - 1], r3.at[step - 1], (s3_s, s3_r), step - 1, peer))
    total = mine(0)
    for step in range(1, NZ):
        three[step - 1].wait_recv()
        total = total + r3[step - 1].astype(F32)
    grad_out[...] = total.astype(BF16)
    for copy in a_copies:
        copy.wait_recv()

    @pl.loop(0, panels)
    def _(c):
        act_out[:, pl.ds(pl.multiple_of(c * bs, bs), bs)] = act_in[table[c]]

    x_copy.wait_recv()
    for copy in one + two + three + a_copies + [x_copy]:
        copy.wait_send()


def weight_kernel(scale, info, tokens, dz, out, turned):
    pair = pl.program_id(0)
    keep, bs = out.shape[1], out.shape[2]
    rows = tokens.shape[0]
    row_blocks = turned.shape[0]

    @pl.when(pair == 0)
    def _():
        @pl.loop(0, row_blocks)
        def _(r):
            turned[r] = tokens[:, pl.ds(pl.multiple_of(r * bs, bs), bs)].T

    for side in range(out.shape[0]):
        value = dz[:, side].reshape(rows, bs)
        for j in range(keep):
            row = info[2 + (out.shape[0] * pair + side) * keep + j]
            out[side, j] = (
                jnp.dot(turned[row], value, preferred_element_type=F32) * scale
            ).astype(BF16)


def per_device(tokens, upstream, blocks, keep_mask, panel_owner):
    tok_dev, width = tokens.shape
    slots, keep, bs, _ = blocks.shape
    panels = panel_owner.shape[0]
    row_blocks = keep_mask.shape[0]
    reps = 2
    me = lax.axis_index("fsdp")
    rep = lax.axis_index("rep")
    shard_ids = jnp.arange(NF, dtype=jnp.int32)
    slot_ids = jnp.arange(slots, dtype=jnp.int32)
    panel_ids = jnp.arange(panels, dtype=jnp.int32)
    member = (panel_owner[:, None] == shard_ids[None, :]).astype(jnp.int32)
    counts = jnp.sum(member, axis=0)
    below = (panel_owner[:, None] < shard_ids[None, :]).astype(jnp.int32)
    first = jnp.sum(below, axis=0)
    send_table = jnp.clip(first[:, None] + slot_ids[None, :], 0, panels - 1).reshape(-1)
    panel_first = jnp.sum(member * first[None, :], axis=1)
    panel_slot = panel_owner * slots + panel_ids - panel_first
    is_mine = (shard_ids == me).astype(jnp.int32)
    own_first = jnp.sum(is_mine * first)
    own_count = jnp.sum(is_mine * counts)
    own_panels = jnp.clip(own_first + slot_ids, 0, panels - 1)
    pick = (panel_ids[None, :] == own_panels[:, None]).astype(jnp.int32)
    running = jnp.cumsum(keep_mask, axis=0)
    own_running = jnp.sum(pick[:, None, :] * running[None, :, :], axis=2)
    keep_ids = jnp.arange(keep, dtype=jnp.int32)
    own_rows = jnp.sum(
        (own_running[:, :, None] <= keep_ids[None, None, :]).astype(jnp.int32), axis=1
    )
    info = jnp.concatenate([jnp.stack([rep, own_count]), own_rows.reshape(-1)]).astype(jnp.int32)

    smem = pl.BlockSpec(memory_space=pltpu.SMEM)
    vmem = pl.BlockSpec(memory_space=pltpu.VMEM)
    dma = lambda n: [pltpu.SemaphoreType.DMA((n,))] * 2
    params = functools.partial(pltpu.CompilerParams, vmem_limit_bytes=VMEM_LIMIT)
    outgoing = pl.pallas_call(
        pick_kernel,
        out_shape=jax.ShapeDtypeStruct((NF, slots, tok_dev, bs), BF16),
        in_specs=[smem, vmem],
        out_specs=vmem,
        compiler_params=params(),
        name="pick_cotangents",
    )(send_table, upstream)
    all_tokens, incoming = pl.pallas_call(
        gather_kernel,
        out_shape=(
            jax.ShapeDtypeStruct((reps, NF, tok_dev, width), BF16),
            jax.ShapeDtypeStruct((NF, slots, tok_dev, bs), BF16),
        ),
        in_specs=[vmem, vmem],
        out_specs=(vmem, vmem),
        scratch_shapes=dma(NZ - 1) + dma(NZ) + dma(NZ) + dma(NZ) + dma(4 * NZ) + dma(NF - 1),
        compiler_params=params(collective_id=0, has_side_effects=True),
        name="gather_tokens",
    )(tokens, outgoing)

    group = NF * tok_dev
    act, dz, part = pl.pallas_call(
        forward_kernel,
        out_shape=(
            jax.ShapeDtypeStruct((NF, slots, tok_dev, bs), BF16),
            jax.ShapeDtypeStruct((slots, group, bs), BF16),
            jax.ShapeDtypeStruct((NF, tok_dev, width), BF16),
        ),
        grid_spec=pltpu.PrefetchScalarGridSpec(
            num_scalar_prefetch=1,
            grid=(slots // 2,),
            in_specs=[
                pl.BlockSpec((1, NF, tok_dev, width), lambda i, s: (s[0], 0, 0, 0)),
                pl.BlockSpec((2, keep, bs, bs), lambda i, s: (i, 0, 0, 0)),
                pl.BlockSpec((NF, 2, tok_dev, bs), lambda i, s: (0, i, 0, 0)),
            ],
            out_specs=[
                pl.BlockSpec((NF, 2, tok_dev, bs), lambda i, s: (0, i, 0, 0)),
                pl.BlockSpec((2, group, bs), lambda i, s: (i, 0, 0)),
                pl.BlockSpec((NF, tok_dev, width), lambda i, s: (0, 0, 0)),
            ],
            scratch_shapes=[
                pltpu.VMEM((width, slots * bs), BF16),
                pltpu.VMEM((group, slots * bs), BF16),
            ],
        ),
        compiler_params=params(),
        name="forward_panels",
    )(info, all_tokens, blocks, incoming)

    dz_both, act_out, input_grad = pl.pallas_call(
        scatter_kernel,
        out_shape=(
            jax.ShapeDtypeStruct((reps, slots, group, bs), BF16),
            jax.ShapeDtypeStruct((tok_dev, panels * bs), BF16),
            jax.ShapeDtypeStruct((tok_dev, width), BF16),
        ),
        in_specs=[smem, vmem, vmem, vmem],
        out_specs=(vmem, vmem, vmem),
        scratch_shapes=[
            pltpu.VMEM((NF * slots, tok_dev, bs), BF16),
            pltpu.VMEM((NY * NZ, tok_dev, width), BF16),
            pltpu.VMEM((NZ, tok_dev, width), BF16),
            pltpu.VMEM((NZ, tok_dev, width), BF16),
            pltpu.VMEM((NZ - 1, tok_dev, width), BF16),
            pltpu.VMEM((NZ - 1, tok_dev, width), BF16),
        ]
        + dma(1) + dma(NF - 1) + dma(NY * NZ) + dma(NZ) + dma(NZ - 1),
        compiler_params=params(collective_id=1, has_side_effects=True),
        name="scatter_results",
    )(panel_slot, dz, act, part)

    scale = 1.0 / math.sqrt(group * reps)
    block_grad = pl.pallas_call(
        functools.partial(weight_kernel, scale),
        out_shape=jax.ShapeDtypeStruct(blocks.shape, BF16),
        grid_spec=pltpu.PrefetchScalarGridSpec(
            num_scalar_prefetch=1,
            grid=(slots // 2,),
            in_specs=[
                pl.BlockSpec((reps * group, width), lambda i, s: (0, 0)),
                pl.BlockSpec((reps, 2, group, bs), lambda i, s: (0, i, 0, 0)),
            ],
            out_specs=pl.BlockSpec((2, keep, bs, bs), lambda i, s: (i, 0, 0, 0)),
            scratch_shapes=[pltpu.VMEM((row_blocks, bs, reps * group), BF16)],
        ),
        compiler_params=params(),
        name="weight_panels",
    )(info, all_tokens.reshape(reps * group, width), dz_both)
    return (act_out, input_grad, block_grad)


def solution(mesh):
    fits = mesh.shape["rep"] == 2 and mesh.shape["fsdp"] == NF
    return jax.shard_map(
        per_device if fits else per_device_general,
        mesh=mesh,
        in_specs=(
            P(("rep", "fsdp"), None),
            P(("rep", "fsdp"), None),
            P("fsdp", None, None, None),
            P(),
            P(),
        ),
        out_specs=(P(("rep", "fsdp"), None), P(("rep", "fsdp"), None), P("fsdp", None, None, None)),
        check_vma=False,
    )
```

```python
import functools
import math

import jax
import jax.numpy as jnp
from jax import lax
from jax.experimental import pallas as pl
from jax.experimental.pallas import tpu as pltpu
from jax.sharding import PartitionSpec as P

BF16 = jnp.bfloat16
F32 = jnp.float32
MESH = pl.DeviceIdType.MESH
VMEM_LIMIT = 60 * 1024 * 1024
NZ, NY, NC = 4, 2, 2
NF = NZ * NY * NC


def per_device_general(tokens, upstream, blocks, keep_mask, panel_owner):
    shard_count = lax.axis_size("fsdp")
    own_index = lax.axis_index("fsdp")
    tok_dev = tokens.shape[0]
    model_width = tokens.shape[1]
    slot_count = blocks.shape[0]
    keep_count = blocks.shape[1]
    block_size = blocks.shape[3]
    row_blocks = keep_mask.shape[0]
    panel_count = panel_owner.shape[0]
    group_rows = tok_dev * shard_count
    rep_count = lax.axis_size("rep")
    shard_ids = jnp.arange(shard_count, dtype=jnp.int32)
    member = (panel_owner[:, None] == shard_ids[None, :]).astype(jnp.int32)
    counts = jnp.sum(member, axis=0)
    first_panel = jnp.cumsum(counts) - counts
    slot_ids = jnp.arange(slot_count, dtype=jnp.int32)
    panel_table = jnp.clip(first_panel[:, None] + slot_ids[None, :], 0, panel_count - 1)
    is_mine = shard_ids == own_index
    own_first = jnp.sum(jnp.where(is_mine, first_panel, 0))
    own_count = jnp.sum(jnp.where(is_mine, counts, 0))
    own_live = slot_ids < own_count
    own_panels = jnp.clip(own_first + slot_ids, 0, panel_count - 1)
    panel_ids = jnp.arange(panel_count, dtype=jnp.int32)
    panel_pick = (panel_ids[None, :] == own_panels[:, None]).astype(jnp.int32)
    running = jnp.cumsum(keep_mask, axis=0)
    own_running = jnp.sum(panel_pick[:, None, :] * running[None, :, :], axis=2)
    pick_ids = jnp.arange(keep_count, dtype=jnp.int32)
    own_rows = jnp.sum(
        (own_running[:, :, None] <= pick_ids[None, None, :]).astype(jnp.int32), axis=1
    )
    upstream_panels = jnp.transpose(upstream.reshape(tok_dev, panel_count, block_size), (1, 0, 2))
    outgoing = jnp.take(upstream_panels, panel_table.reshape(-1), axis=0)
    incoming = lax.all_to_all(outgoing, "fsdp", split_axis=0, concat_axis=1, tiled=True)
    group_tokens = lax.all_gather(tokens, "fsdp", axis=0, tiled=True)
    all_tokens = lax.all_gather(group_tokens, "rep", axis=0, tiled=True)
    token_blocks = jnp.transpose(all_tokens).reshape(row_blocks, block_size, rep_count * group_rows)

    dense_panels = jnp.zeros((slot_count, row_blocks, block_size, block_size), blocks.dtype)
    dense_panels = dense_panels.at[slot_ids[:, None], own_rows].set(blocks)
    dense = dense_panels.reshape(slot_count, model_width, block_size)
    preact = lax.dot_general(
        group_tokens, dense, (((1,), (1,)), ((), ())), preferred_element_type=jnp.float32
    )
    sigmoid_z = jax.nn.sigmoid(preact)
    activations = (preact * sigmoid_z).astype(jnp.bfloat16)
    slope = sigmoid_z * (1.0 + preact * (1.0 - sigmoid_z))
    cot = jnp.transpose(incoming, (1, 0, 2)).astype(jnp.float32)
    dpre = jnp.where(own_live[None, :, None], cot * slope, 0.0).astype(jnp.bfloat16)
    dpre_all = lax.all_gather(dpre, "rep", axis=0, tiled=True)
    backward = lax.dot_general(
        dpre, dense, (((1, 2), (0, 2)), ((), ())), preferred_element_type=jnp.float32
    )
    input_grad = lax.psum_scatter(
        backward, "fsdp", scatter_dimension=0, tiled=True
    ).astype(jnp.bfloat16)
    returned = lax.all_to_all(activations, "fsdp", split_axis=0, concat_axis=1, tiled=True)
    panel_first = jnp.sum(member * first_panel[None, :], axis=1)
    panel_slot = panel_owner * slot_count + panel_ids - panel_first
    act_panels = jnp.take(returned, panel_slot, axis=1)
    activation_out = act_panels.reshape(tok_dev, panel_count * block_size)
    scale = 1.0 / math.sqrt(group_rows * rep_count)

    def panel_step(nothing, item):
        row_ids, dz = item
        chosen = jnp.take(token_blocks, row_ids, axis=0)
        grad = lax.dot_general(
            chosen, dz, (((2,), (0,)), ((), ())), preferred_element_type=jnp.float32
        )
        return nothing, (grad * scale).astype(jnp.bfloat16)

    nothing, block_grad = lax.scan(
        panel_step, jnp.zeros((), jnp.float32), (own_rows, jnp.transpose(dpre_all, (1, 0, 2)))
    )
    return (activation_out, input_grad, block_grad)


class Place:
    def __init__(self):
        self.rep = lax.axis_index("rep")
        self.me = lax.axis_index("fsdp")
        self.core = self.me % NC
        self.y = (self.me // NC) % NY
        self.z = self.me // (NC * NY)

    def at(self, z, y, core):
        return (z * NY + y) * NC + core

    def z_back(self, step):
        return (self.z + NZ - step) % NZ

    def z_ahead(self, step):
        return (self.z + step) % NZ

    def fsdp_peer(self, step):
        return (self.me + step) % NF

    def greet(self):
        barrier = pltpu.get_barrier_semaphore()
        for step in range(1, NF):
            pl.semaphore_signal(
                barrier, inc=1, device_id=(self.rep, self.fsdp_peer(step)), device_id_type=MESH
            )
        pl.semaphore_signal(barrier, inc=1, device_id=(1 - self.rep, self.me), device_id_type=MESH)
        pl.semaphore_wait(barrier, NF)


def send(src, dst, sems, slot, device):
    send_sems, recv_sems = sems
    copy = pltpu.make_async_remote_copy(
        src_ref=src,
        dst_ref=dst,
        send_sem=send_sems.at[slot],
        recv_sem=recv_sems.at[slot],
        device_id=device,
        device_id_type=MESH,
    )
    copy.start()
    return copy


def layer_kernel(
    scale,
    first, owner, keep, tokens, upstream, blocks_hbm,
    act_out, grad_out, block_grad,
    all_tokens, turned, dense, blocks, grads, up3, outgoing, incoming,
    act, act_in, dz_both, dz_flat, part, r1, s2, r2, s3, r3, run, place_of, kept_row,
    local, z_s, z_r, y_s, y_r, x_s, x_r, d_s, d_r, c_s, c_r, u_s, u_r,
    v_s, v_r, a_s, a_r, p_s, p_r, q_s, q_r, t_s, t_r,
):
    place = Place()
    rep, me, z, y, core = place.rep, place.me, place.z, place.y, place.core
    slots, bs = outgoing.shape[1], outgoing.shape[3]
    row_blocks, panels = keep.shape
    kept = block_grad.shape[1]
    tok_dev, width = tokens.shape
    rows = NF * tok_dev
    pairs = slots // 2
    y_peer = (rep, place.at(z, 1 - y, core))
    x_peer = (1 - rep, me)
    core_peer = (rep, place.at(z, y, 1 - core))
    z_sems, y_sems, x_sems = (z_s, z_r), (y_s, y_r), (x_s, x_r)
    d_sems, c_sems, u_sems = (d_s, d_r), (c_s, c_r), (u_s, u_r)
    early = pairs // 2 + 1
    halves = ((0, 2 * early), (2 * early, slots - 2 * early))

    load_blocks = pltpu.make_async_copy(
        blocks_hbm, blocks.at[pl.ds(0, slots * kept)], local.at[0]
    )
    load_blocks.start()
    all_tokens[rep, me] = tokens[...]
    place.greet()

    own = all_tokens.at[rep, me]
    z_copies = {}
    for step in range(1, NZ):
        peer = (rep, place.at(place.z_ahead(step), y, core))
        z_copies[step] = send(own, own, z_sems, step - 1, peer)
    y_copies, x_copies, d_copies, c_copies = [], [], [None] * NZ, [None] * (4 * NZ)

    def spread(step):
        piece = all_tokens.at[rep, place.at(place.z_back(step), y, core)]
        y_copies.append(send(piece, piece, y_sems, step, y_peer))
        x_copies.append(send(piece, piece, x_sems, step, x_peer))
        c_copies[step] = send(piece, piece, c_sems, step, core_peer)

    spread(0)

    for c in range(panels):
        up3[c] = upstream[:, c * bs:(c + 1) * bs]
    u_copies = [[], []]
    for half, (start, size) in enumerate(halves):
        @pl.loop(0, NF)
        def _(k):
            for p in range(start, start + size):
                outgoing[k, p] = up3[jnp.minimum(first[k] + p, panels - 1)]

        for step in range(1, NF):
            peer = place.fsdp_peer(step)
            span = pl.ds(start, size)
            u_copies[half].append(send(
                outgoing.at[peer, span], incoming.at[me, span], u_sems,
                half * (NF - 1) + step - 1, (rep, peer),
            ))
    incoming[me] = outgoing[me]

    @pl.loop(0, slots)
    def _(p):
        c = jnp.minimum(first[me] + p, panels - 1)
        count = jnp.int32(0)
        for r in range(row_blocks):
            bit = keep[r, c]
            count = count + bit
            run[p * row_blocks + r] = count
            place_of[p * row_blocks + r] = jnp.where(
                bit == 1, p * kept + jnp.clip(count - 1, 0, kept - 1), slots * kept
            )

    blocks[slots * kept] = jnp.zeros((bs, bs), BF16)
    load_blocks.wait()

    def build(start, stop):
        @pl.loop(start, stop)
        def _(i):
            for side in range(2):
                for r in range(row_blocks):
                    at = place_of[(2 * i + side) * row_blocks + r]
                    dense[i, r * bs:(r + 1) * bs, side * bs:(side + 1) * bs] = blocks[at]

    for step in range(1, NZ):
        z_copies[step].wait_recv()
        spread(step)
        build(step - 1, step)
    for step in range(NZ):
        f_x = place.at(place.z_back(step), y, core)
        f_y = place.at(place.z_back(step), 1 - y, core)
        y_copies[step].wait_recv()
        piece = all_tokens.at[rep, f_y]
        c_copies[2 * NZ + step] = send(piece, piece, c_sems, 2 * NZ + step, core_peer)
        if step % 2 == 1:
            d_copies[step] = send(piece, piece, d_sems, step, x_peer)
        x_copies[step].wait_recv()
        piece = all_tokens.at[1 - rep, f_x]
        if step % 2 == 0:
            d_copies[step] = send(piece, piece, d_sems, step, y_peer)
        c_copies[NZ + step] = send(piece, piece, c_sems, NZ + step, core_peer)
        build(NZ - 1 + step, NZ + step)

    @pl.loop(0, slots)
    def _(p):
        @pl.loop(0, kept)
        def _(j):
            row = jnp.int32(0)
            for r in range(row_blocks):
                row = row + jnp.where(run[p * row_blocks + r] <= j, 1, 0)
            kept_row[p * kept + j] = jnp.minimum(row, row_blocks - 1)

    for step in range(NZ):
        c_copies[step].wait_recv()
        c_copies[2 * NZ + step].wait_recv()

    count = first[me + 1] - first[me]
    v_copies, a_copies = [], []
    for half, (start, size) in enumerate(halves):
        for copy in u_copies[half]:
            copy.wait_recv()

        @pl.loop(start // 2, (start + size) // 2)
        def _(i):
            preact = jnp.dot(
                all_tokens[rep].reshape(rows, width), dense[i], preferred_element_type=F32
            )
            for side in range(2):
                slot = 2 * i + side
                zed = preact[:, side * bs:(side + 1) * bs]
                sig = jax.nn.sigmoid(zed)
                act[:, slot] = (zed * sig).astype(BF16).reshape(NF, tok_dev, bs)
                slope = sig * (1.0 + zed * (1.0 - sig))
                cot = incoming[:, slot].reshape(rows, bs).astype(F32)
                value = jnp.where(slot < count, cot * slope, 0.0).astype(BF16)
                dz_both[rep, slot] = value
                dz_flat[i, :, side * bs:(side + 1) * bs] = value

        span = pl.ds(start, size)
        piece = dz_both.at[rep, span]
        v_copies.append(send(piece, piece, (v_s, v_r), half, x_peer))
        for step in range(1, NF):
            peer = place.fsdp_peer(step)
            a_copies.append(send(
                act.at[peer, span], act_in.at[pl.ds(me * slots + start, size)], (a_s, a_r),
                half * (NF - 1) + step - 1, (rep, peer),
            ))
        if half == 0:
            for step in range(NZ):
                d_copies[step].wait_recv()
                piece = all_tokens.at[1 - rep, place.at(place.z_back(step), 1 - y, core)]
                c_copies[3 * NZ + step] = send(piece, piece, c_sems, 3 * NZ + step, core_peer)
    act_in[pl.ds(me * slots, slots)] = act[me]

    chunks = 4
    chunk = width // chunks
    p_copies, q_copies, t_copies = [], [], []
    for n in range(chunks):
        span = pl.ds(n * chunk, chunk)
        total = jnp.zeros((rows, chunk), F32)
        for i in range(pairs):
            total = total + lax.dot_general(
                dz_flat[i], dense[i, span, :], (((1,), (1,)), ((), ())),
                preferred_element_type=F32,
            )
        part[:, :, :, :, span] = total.astype(BF16).reshape(NZ, NY, NC, tok_dev, chunk)
        p_copies.append(send(
            part.at[:, :, 1 - core, :, span], r1.at[:, :, :, span], (p_s, p_r), n, core_peer
        ))
    for n in range(chunks):
        span = pl.ds(n * chunk, chunk)
        p_copies[n].wait_recv()
        s2[:, :, span] = (
            part[:, 1 - y, core, :, span].astype(F32) + r1[:, 1 - y, :, span].astype(F32)
        ).astype(BF16)
        q_copies.append(send(s2.at[:, :, span], r2.at[:, :, span], (q_s, q_r), n, y_peer))

    def column_sum(at_z, span):
        return (
            part[at_z, y, core, :, span].astype(F32)
            + r1[at_z, y, :, span].astype(F32)
            + r2[at_z, :, span].astype(F32)
        )

    def to_z(n):
        span = pl.ds(n * chunk, chunk)
        q_copies[n].wait_recv()
        for step in range(1, NZ):
            s3[step - 1, :, span] = column_sum(place.z_ahead(step), span).astype(BF16)
            peer = (rep, place.at(place.z_ahead(step), y, core))
            t_copies.append(send(
                s3.at[step - 1, :, span], r3.at[step - 1, :, span], (t_s, t_r),
                n * (NZ - 1) + step - 1, peer,
            ))

    stores = []

    def weight(start, size):
        @pl.loop(start, start + size)
        def _(p):
            value = dz_both[:, p].reshape(2 * rows, bs)
            for j in range(kept):
                grads[p, j] = (
                    jnp.dot(
                        turned[kept_row[p * kept + j]], value, preferred_element_type=F32
                    ) * scale
                ).astype(BF16)

        span = pl.ds(start, size)
        stores.append(pltpu.make_async_copy(
            grads.at[span], block_grad.at[span], local.at[1 + len(stores)]
        ))
        stores[-1].start()

    for step in range(NZ):
        c_copies[NZ + step].wait_recv()
        c_copies[3 * NZ + step].wait_recv()

    @pl.loop(0, row_blocks)
    def _(r):
        lanes = pl.ds(pl.multiple_of(r * bs, bs), bs)
        turned[r] = all_tokens[:, :, :, lanes].reshape(2 * rows, bs).T

    v_copies[0].wait_recv()
    cut = halves[0][1] // 2
    to_z(0)
    weight(0, cut)
    to_z(1)
    to_z(2)
    weight(cut, halves[0][1] - cut)
    to_z(3)
    v_copies[1].wait_recv()
    weight(*halves[1])
    for n in range(chunks):
        span = pl.ds(n * chunk, chunk)
        total = column_sum(z, span)
        for step in range(1, NZ):
            t_copies[n * (NZ - 1) + step - 1].wait_recv()
            total = total + r3[step - 1, :, span].astype(F32)
        grad_out[:, span] = total.astype(BF16)
    for copy in a_copies:
        copy.wait_recv()

    @pl.loop(0, panels)
    def _(c):
        k = owner[c]
        at = jnp.clip(k * slots + c - first[k], 0, NF * slots - 1)
        act_out[:, pl.ds(pl.multiple_of(c * bs, bs), bs)] = act_in[at]

    for store in stores:
        store.wait()
    sent = list(z_copies.values()) + y_copies + x_copies + d_copies + c_copies + u_copies[0]
    sent += u_copies[1] + v_copies + a_copies + p_copies + q_copies + t_copies
    for copy in sent:
        copy.wait_send()


def per_device(tokens, upstream, blocks, keep_mask, panel_owner):
    tok_dev, width = tokens.shape
    slots, keep, bs, _ = blocks.shape
    panels = panel_owner.shape[0]
    row_blocks = keep_mask.shape[0]
    reps = 2
    group = NF * tok_dev
    pairs = slots // 2
    shard_ids = jnp.arange(NF + 1, dtype=jnp.int32)
    below = (panel_owner[:, None] < shard_ids[None, :]).astype(jnp.int32)
    first = jnp.sum(below, axis=0)

    smem = pl.BlockSpec(memory_space=pltpu.SMEM)
    vmem = pl.BlockSpec(memory_space=pltpu.VMEM)
    anywhere = pl.BlockSpec(memory_space=pl.ANY)
    dma = lambda n: [pltpu.SemaphoreType.DMA((n,))] * 2
    act_out, input_grad, block_grad = pl.pallas_call(
        functools.partial(layer_kernel, 1.0 / math.sqrt(group * reps)),
        out_shape=(
            jax.ShapeDtypeStruct((tok_dev, panels * bs), BF16),
            jax.ShapeDtypeStruct((tok_dev, width), BF16),
            jax.ShapeDtypeStruct((slots, keep, bs, bs), BF16),
        ),
        in_specs=[smem, smem, smem, vmem, vmem, anywhere],
        out_specs=(vmem, vmem, anywhere),
        scratch_shapes=[
            pltpu.VMEM((reps, NF, tok_dev, width), BF16),
            pltpu.VMEM((row_blocks, bs, reps * group), BF16),
            pltpu.VMEM((pairs, width, 2 * bs), BF16),
            pltpu.VMEM((slots * keep + 1, bs, bs), BF16),
            pltpu.VMEM((slots, keep, bs, bs), BF16),
            pltpu.VMEM((panels, tok_dev, bs), BF16),
            pltpu.VMEM((NF, slots, tok_dev, bs), BF16),
            pltpu.VMEM((NF, slots, tok_dev, bs), BF16),
            pltpu.VMEM((NF, slots, tok_dev, bs), BF16),
            pltpu.VMEM((NF * slots, tok_dev, bs), BF16),
            pltpu.VMEM((reps, slots, group, bs), BF16),
            pltpu.VMEM((pairs, group, 2 * bs), BF16),
            pltpu.VMEM((NZ, NY, NC, tok_dev, width), BF16),
            pltpu.VMEM((NZ, NY, tok_dev, width), BF16),
            pltpu.VMEM((NZ, tok_dev, width), BF16),
            pltpu.VMEM((NZ, tok_dev, width), BF16),
            pltpu.VMEM((NZ - 1, tok_dev, width), BF16),
            pltpu.VMEM((NZ - 1, tok_dev, width), BF16),
            pltpu.SMEM((slots * row_blocks,), jnp.int32),
            pltpu.SMEM((slots * row_blocks,), jnp.int32),
            pltpu.SMEM((slots * keep,), jnp.int32),
            pltpu.SemaphoreType.DMA((8,)),
        ]
        + dma(NZ - 1) + dma(NZ) + dma(NZ) + dma(NZ) + dma(4 * NZ) + dma(2 * (NF - 1))
        + dma(2) + dma(2 * (NF - 1)) + dma(4) + dma(4) + dma(4 * (NZ - 1)),
        compiler_params=pltpu.CompilerParams(
            collective_id=0, has_side_effects=True, vmem_limit_bytes=VMEM_LIMIT
        ),
        name="layer",
    )(first, panel_owner, keep_mask, tokens, upstream, blocks.reshape(slots * keep, bs, bs))
    return (act_out, input_grad, block_grad)


def solution(mesh):
    fits = mesh.shape["rep"] == 2 and mesh.shape["fsdp"] == NF
    return jax.shard_map(
        per_device if fits else per_device_general,
        mesh=mesh,
        in_specs=(
            P(("rep", "fsdp"), None),
            P(("rep", "fsdp"), None),
            P("fsdp", None, None, None),
            P(),
            P(),
        ),
        out_specs=(P(("rep", "fsdp"), None), P(("rep", "fsdp"), None), P("fsdp", None, None, None)),
        check_vma=False,
    )
```

```python
import functools
import math

import jax
import jax.numpy as jnp
from jax import lax
from jax.experimental import pallas as pl
from jax.experimental.pallas import tpu as pltpu
from jax.sharding import PartitionSpec as P

BF16 = jnp.bfloat16
F32 = jnp.float32
MESH = pl.DeviceIdType.MESH
VMEM_LIMIT = 60 * 1024 * 1024
NZ, NY, NC = 4, 2, 2
NF = NZ * NY * NC


def per_device_general(tokens, upstream, blocks, keep_mask, panel_owner):
    shard_count = lax.axis_size("fsdp")
    own_index = lax.axis_index("fsdp")
    tok_dev = tokens.shape[0]
    model_width = tokens.shape[1]
    slot_count = blocks.shape[0]
    keep_count = blocks.shape[1]
    block_size = blocks.shape[3]
    row_blocks = keep_mask.shape[0]
    panel_count = panel_owner.shape[0]
    group_rows = tok_dev * shard_count
    rep_count = lax.axis_size("rep")
    shard_ids = jnp.arange(shard_count, dtype=jnp.int32)
    member = (panel_owner[:, None] == shard_ids[None, :]).astype(jnp.int32)
    counts = jnp.sum(member, axis=0)
    first_panel = jnp.cumsum(counts) - counts
    slot_ids = jnp.arange(slot_count, dtype=jnp.int32)
    panel_table = jnp.clip(first_panel[:, None] + slot_ids[None, :], 0, panel_count - 1)
    is_mine = shard_ids == own_index
    own_first = jnp.sum(jnp.where(is_mine, first_panel, 0))
    own_count = jnp.sum(jnp.where(is_mine, counts, 0))
    own_live = slot_ids < own_count
    own_panels = jnp.clip(own_first + slot_ids, 0, panel_count - 1)
    panel_ids = jnp.arange(panel_count, dtype=jnp.int32)
    panel_pick = (panel_ids[None, :] == own_panels[:, None]).astype(jnp.int32)
    running = jnp.cumsum(keep_mask, axis=0)
    own_running = jnp.sum(panel_pick[:, None, :] * running[None, :, :], axis=2)
    pick_ids = jnp.arange(keep_count, dtype=jnp.int32)
    own_rows = jnp.sum(
        (own_running[:, :, None] <= pick_ids[None, None, :]).astype(jnp.int32), axis=1
    )
    upstream_panels = jnp.transpose(upstream.reshape(tok_dev, panel_count, block_size), (1, 0, 2))
    outgoing = jnp.take(upstream_panels, panel_table.reshape(-1), axis=0)
    incoming = lax.all_to_all(outgoing, "fsdp", split_axis=0, concat_axis=1, tiled=True)
    group_tokens = lax.all_gather(tokens, "fsdp", axis=0, tiled=True)
    all_tokens = lax.all_gather(group_tokens, "rep", axis=0, tiled=True)
    token_blocks = jnp.transpose(all_tokens).reshape(row_blocks, block_size, rep_count * group_rows)

    dense_panels = jnp.zeros((slot_count, row_blocks, block_size, block_size), blocks.dtype)
    dense_panels = dense_panels.at[slot_ids[:, None], own_rows].set(blocks)
    dense = dense_panels.reshape(slot_count, model_width, block_size)
    preact = lax.dot_general(
        group_tokens, dense, (((1,), (1,)), ((), ())), preferred_element_type=jnp.float32
    )
    sigmoid_z = jax.nn.sigmoid(preact)
    activations = (preact * sigmoid_z).astype(jnp.bfloat16)
    slope = sigmoid_z * (1.0 + preact * (1.0 - sigmoid_z))
    cot = jnp.transpose(incoming, (1, 0, 2)).astype(jnp.float32)
    dpre = jnp.where(own_live[None, :, None], cot * slope, 0.0).astype(jnp.bfloat16)
    dpre_all = lax.all_gather(dpre, "rep", axis=0, tiled=True)
    backward = lax.dot_general(
        dpre, dense, (((1, 2), (0, 2)), ((), ())), preferred_element_type=jnp.float32
    )
    input_grad = lax.psum_scatter(
        backward, "fsdp", scatter_dimension=0, tiled=True
    ).astype(jnp.bfloat16)
    returned = lax.all_to_all(activations, "fsdp", split_axis=0, concat_axis=1, tiled=True)
    panel_first = jnp.sum(member * first_panel[None, :], axis=1)
    panel_slot = panel_owner * slot_count + panel_ids - panel_first
    act_panels = jnp.take(returned, panel_slot, axis=1)
    activation_out = act_panels.reshape(tok_dev, panel_count * block_size)
    scale = 1.0 / math.sqrt(group_rows * rep_count)

    def panel_step(nothing, item):
        row_ids, dz = item
        chosen = jnp.take(token_blocks, row_ids, axis=0)
        grad = lax.dot_general(
            chosen, dz, (((2,), (0,)), ((), ())), preferred_element_type=jnp.float32
        )
        return nothing, (grad * scale).astype(jnp.bfloat16)

    nothing, block_grad = lax.scan(
        panel_step, jnp.zeros((), jnp.float32), (own_rows, jnp.transpose(dpre_all, (1, 0, 2)))
    )
    return (activation_out, input_grad, block_grad)


class Place:
    def __init__(self):
        self.rep = lax.axis_index("rep")
        self.me = lax.axis_index("fsdp")
        self.core = self.me % NC
        self.y = (self.me // NC) % NY
        self.z = self.me // (NC * NY)

    def at(self, z, y, core):
        return (z * NY + y) * NC + core

    def z_back(self, step):
        return (self.z + NZ - step) % NZ

    def z_ahead(self, step):
        return (self.z + step) % NZ

    def fsdp_peer(self, step):
        return (self.me + step) % NF

    def greet(self):
        barrier = pltpu.get_barrier_semaphore()
        for step in range(1, NF):
            pl.semaphore_signal(
                barrier, inc=1, device_id=(self.rep, self.fsdp_peer(step)), device_id_type=MESH
            )
        pl.semaphore_signal(barrier, inc=1, device_id=(1 - self.rep, self.me), device_id_type=MESH)
        pl.semaphore_wait(barrier, NF)


def send(src, dst, sems, slot, device):
    send_sems, recv_sems = sems
    copy = pltpu.make_async_remote_copy(
        src_ref=src,
        dst_ref=dst,
        send_sem=send_sems.at[slot],
        recv_sem=recv_sems.at[slot],
        device_id=device,
        device_id_type=MESH,
    )
    copy.start()
    return copy


def layer_kernel(
    scale,
    first, keep, tokens, upstream, blocks_hbm,
    act_in, grad_out, early_grads, turned_out, dz_late, kept_row,
    all_tokens, turned, dense, blocks, grads, up3, outgoing, incoming,
    act, slope, dz_both, dz_flat, part, r1, s2, r2, s3, r3, run, place_of,
    local, z_s, z_r, y_s, y_r, x_s, x_r, d_s, d_r, c_s, c_r, u_s, u_r,
    v_s, v_r, a_s, a_r, p_s, p_r, q_s, q_r, t_s, t_r,
):
    place = Place()
    rep, me, z, y, core = place.rep, place.me, place.z, place.y, place.core
    slots, bs = outgoing.shape[1], outgoing.shape[3]
    row_blocks, panels = keep.shape
    kept = early_grads.shape[1]
    tok_dev, width = tokens.shape
    rows = NF * tok_dev
    pairs = slots // 2
    y_peer = (rep, place.at(z, 1 - y, core))
    x_peer = (1 - rep, me)
    core_peer = (rep, place.at(z, y, 1 - core))
    z_sems, y_sems, x_sems = (z_s, z_r), (y_s, y_r), (x_s, x_r)
    d_sems, c_sems, u_sems = (d_s, d_r), (c_s, c_r), (u_s, u_r)
    early = pairs // 2 + 1
    halves = ((0, 2 * early), (2 * early, slots - 2 * early))

    load_blocks = pltpu.make_async_copy(
        blocks_hbm, blocks.at[pl.ds(0, slots * kept)], local.at[0]
    )
    load_blocks.start()
    all_tokens[rep, me] = tokens[...]
    place.greet()

    own = all_tokens.at[rep, me]
    z_copies = {}
    for step in range(1, NZ):
        peer = (rep, place.at(place.z_ahead(step), y, core))
        z_copies[step] = send(own, own, z_sems, step - 1, peer)
    y_copies, x_copies, d_copies, c_copies = [], [], [None] * NZ, [None] * (4 * NZ)

    def spread(step):
        piece = all_tokens.at[rep, place.at(place.z_back(step), y, core)]
        y_copies.append(send(piece, piece, y_sems, step, y_peer))
        x_copies.append(send(piece, piece, x_sems, step, x_peer))
        c_copies[step] = send(piece, piece, c_sems, step, core_peer)

    spread(0)

    for c in range(panels):
        up3[c] = upstream[:, c * bs:(c + 1) * bs]
    u_copies = [[], []]
    for half, (start, size) in enumerate(halves):
        @pl.loop(0, NF)
        def _(k):
            for p in range(start, start + size):
                outgoing[k, p] = up3[jnp.minimum(first[k] + p, panels - 1)]

        for step in range(1, NF):
            peer = place.fsdp_peer(step)
            span = pl.ds(start, size)
            u_copies[half].append(send(
                outgoing.at[peer, span], incoming.at[me, span], u_sems,
                half * (NF - 1) + step - 1, (rep, peer),
            ))
    incoming[me] = outgoing[me]

    @pl.loop(0, slots)
    def _(p):
        c = jnp.minimum(first[me] + p, panels - 1)
        count = jnp.int32(0)
        for r in range(row_blocks):
            bit = keep[r, c]
            count = count + bit
            run[p * row_blocks + r] = count
            place_of[p * row_blocks + r] = jnp.where(
                bit == 1, p * kept + jnp.clip(count - 1, 0, kept - 1), slots * kept
            )

    blocks[slots * kept] = jnp.zeros((bs, bs), BF16)
    load_blocks.wait()

    def build(start, stop):
        @pl.loop(start, stop)
        def _(i):
            for side in range(2):
                for r in range(row_blocks):
                    at = place_of[(2 * i + side) * row_blocks + r]
                    dense[i, r * bs:(r + 1) * bs, side * bs:(side + 1) * bs] = blocks[at]

    for step in range(1, NZ):
        z_copies[step].wait_recv()
        spread(step)
        build(step - 1, step)
    for step in range(NZ):
        f_x = place.at(place.z_back(step), y, core)
        f_y = place.at(place.z_back(step), 1 - y, core)
        y_copies[step].wait_recv()
        piece = all_tokens.at[rep, f_y]
        c_copies[2 * NZ + step] = send(piece, piece, c_sems, 2 * NZ + step, core_peer)
        if step % 2 == 1:
            d_copies[step] = send(piece, piece, d_sems, step, x_peer)
        x_copies[step].wait_recv()
        piece = all_tokens.at[1 - rep, f_x]
        if step % 2 == 0:
            d_copies[step] = send(piece, piece, d_sems, step, y_peer)
        c_copies[NZ + step] = send(piece, piece, c_sems, NZ + step, core_peer)
        build(NZ - 1 + step, NZ + step)

    @pl.loop(0, slots)
    def _(p):
        @pl.loop(0, kept)
        def _(j):
            row = jnp.int32(0)
            for r in range(row_blocks):
                row = row + jnp.where(run[p * row_blocks + r] <= j, 1, 0)
            kept_row[p * kept + j] = jnp.minimum(row, row_blocks - 1)

    for step in range(NZ):
        c_copies[step].wait_recv()
        c_copies[2 * NZ + step].wait_recv()

    count = first[me + 1] - first[me]
    v_copies, a_copies = [], []
    for half, (start, size) in enumerate(halves):
        @pl.loop(start // 2, (start + size) // 2)
        def _(i):
            preact = jnp.dot(
                all_tokens[rep].reshape(rows, width), dense[i], preferred_element_type=F32
            )
            for side in range(2):
                slot = 2 * i + side
                zed = preact[:, side * bs:(side + 1) * bs]
                sig = jax.nn.sigmoid(zed)
                act[:, slot] = (zed * sig).astype(BF16).reshape(NF, tok_dev, bs)
                slope[slot] = sig * (1.0 + zed * (1.0 - sig))

        span = pl.ds(start, size)
        for step in range(1, NF):
            peer = place.fsdp_peer(step)
            a_copies.append(send(
                act.at[peer, span], act_in.at[pl.ds(me * slots + start, size)], (a_s, a_r),
                half * (NF - 1) + step - 1, (rep, peer),
            ))
        if half == 0:
            for step in range(NZ):
                d_copies[step].wait_recv()
                piece = all_tokens.at[1 - rep, place.at(place.z_back(step), 1 - y, core)]
                c_copies[3 * NZ + step] = send(piece, piece, c_sems, 3 * NZ + step, core_peer)
    act_in[pl.ds(me * slots, slots)] = act[me]

    def turn(group):
        @pl.loop(0, row_blocks)
        def _(r):
            lanes = pl.ds(pl.multiple_of(r * bs, bs), bs)
            span = pl.ds(pl.multiple_of(group * rows, rows), rows)
            turned[r, :, span] = all_tokens[group, :, :, lanes].reshape(rows, bs).T

    turn(rep)
    for half, (start, size) in enumerate(halves):
        for copy in u_copies[half]:
            copy.wait_recv()

        @pl.loop(start // 2, (start + size) // 2)
        def _(i):
            for side in range(2):
                slot = 2 * i + side
                cot = incoming[:, slot].reshape(rows, bs).astype(F32)
                value = jnp.where(slot < count, cot * slope[slot], 0.0).astype(BF16)
                dz_both[rep, slot] = value
                dz_flat[i, :, side * bs:(side + 1) * bs] = value

        piece = dz_both.at[rep, pl.ds(start, size)]
        v_copies.append(send(piece, piece, (v_s, v_r), half, x_peer))

    chunks = 4
    chunk = width // chunks
    p_copies, q_copies, t_copies = [], [], []
    for n in range(chunks):
        span = pl.ds(n * chunk, chunk)
        total = jnp.zeros((rows, chunk), F32)
        for i in range(pairs):
            total = total + lax.dot_general(
                dz_flat[i], dense[i, span, :], (((1,), (1,)), ((), ())),
                preferred_element_type=F32,
            )
        part[:, :, :, :, span] = total.astype(BF16).reshape(NZ, NY, NC, tok_dev, chunk)
        p_copies.append(send(
            part.at[:, :, 1 - core, :, span], r1.at[:, :, :, span], (p_s, p_r), n, core_peer
        ))
    for n in range(chunks):
        span = pl.ds(n * chunk, chunk)
        p_copies[n].wait_recv()
        s2[:, :, span] = (
            part[:, 1 - y, core, :, span].astype(F32) + r1[:, 1 - y, :, span].astype(F32)
        ).astype(BF16)
        q_copies.append(send(s2.at[:, :, span], r2.at[:, :, span], (q_s, q_r), n, y_peer))

    def column_sum(at_z, span):
        return (
            part[at_z, y, core, :, span].astype(F32)
            + r1[at_z, y, :, span].astype(F32)
            + r2[at_z, :, span].astype(F32)
        )

    def to_z(n):
        span = pl.ds(n * chunk, chunk)
        q_copies[n].wait_recv()
        for step in range(1, NZ):
            s3[step - 1, :, span] = column_sum(place.z_ahead(step), span).astype(BF16)
            peer = (rep, place.at(place.z_ahead(step), y, core))
            t_copies.append(send(
                s3.at[step - 1, :, span], r3.at[step - 1, :, span], (t_s, t_r),
                n * (NZ - 1) + step - 1, peer,
            ))

    stores = []

    def store(src, dst):
        copy = pltpu.make_async_copy(src, dst, local.at[1 + len(stores)])
        copy.start()
        stores.append(copy)

    def weight(start, size):
        @pl.loop(start, start + size)
        def _(p):
            weight_panel(scale, kept_row, p * kept, turned, dz_both[:, p], grads, p)

        span = pl.ds(start, size)
        store(grads.at[span], early_grads.at[span])

    for step in range(NZ):
        c_copies[NZ + step].wait_recv()
        c_copies[3 * NZ + step].wait_recv()
    turn(1 - rep)
    store(turned, turned_out)
    to_z(0)
    to_z(1)
    v_copies[0].wait_recv()
    cut = halves[0][1] // 2
    weight(0, cut)
    to_z(2)
    to_z(3)
    weight(cut, halves[0][1] - cut)
    v_copies[1].wait_recv()
    store(dz_both.at[:, pl.ds(*halves[1])], dz_late)
    for n in range(chunks):
        span = pl.ds(n * chunk, chunk)
        total = column_sum(z, span)
        for step in range(1, NZ):
            t_copies[n * (NZ - 1) + step - 1].wait_recv()
            total = total + r3[step - 1, :, span].astype(F32)
        grad_out[:, span] = total.astype(BF16)
    for copy in a_copies:
        copy.wait_recv()
    for copy in stores:
        copy.wait()
    sent = list(z_copies.values()) + y_copies + x_copies + d_copies + c_copies + u_copies[0]
    sent += u_copies[1] + v_copies + a_copies + p_copies + q_copies + t_copies
    for copy in sent:
        copy.wait_send()


def weight_panel(scale, kept_row, base, turned, dz, out, at):
    bs = dz.shape[-1]
    value = dz.reshape(-1, bs)
    for j in range(0, out.shape[1], 4):
        chosen = jnp.concatenate([turned[kept_row[base + j + t]] for t in range(4)], axis=0)
        grad = jnp.dot(chosen, value, preferred_element_type=F32) * scale
        out[at, j:j + 4] = grad.astype(BF16).reshape(4, bs, bs)


def finish_kernel(
    scale,
    first, owner, kept_row, act_in, grad_in, early_grads, turned_hbm, dz_hbm,
    act_out, grad_out, block_grad,
    turned, dz, grads, sems,
):
    early, kept = early_grads.shape[:2]
    late = grads.shape[0]
    slots = early + late
    bs = turned.shape[1]
    panels = act_out.shape[1] // bs
    loads = [
        pltpu.make_async_copy(dz_hbm, dz, sems.at[0]),
        pltpu.make_async_copy(turned_hbm, turned, sems.at[1]),
    ]
    for copy in loads:
        copy.start()
    stores = []
    for s in range(early):
        stores.append(pltpu.make_async_copy(early_grads.at[s], block_grad.at[s], sems.at[2 + s]))
        stores[-1].start()
    grad_out[...] = grad_in[...]

    @pl.loop(0, panels)
    def _(c):
        k = owner[c]
        at = jnp.clip(k * slots + c - first[k], 0, NF * slots - 1)
        act_out[:, pl.ds(pl.multiple_of(c * bs, bs), bs)] = act_in[at]

    for copy in loads:
        copy.wait()
    for s in range(late):
        weight_panel(scale, kept_row, (early + s) * kept, turned, dz[:, s], grads, s)
        stores.append(
            pltpu.make_async_copy(grads.at[s], block_grad.at[early + s], sems.at[2 + early + s])
        )
        stores[-1].start()
    for copy in stores:
        copy.wait()


def per_device(tokens, upstream, blocks, keep_mask, panel_owner):
    tok_dev, width = tokens.shape
    slots, keep, bs, _ = blocks.shape
    panels = panel_owner.shape[0]
    row_blocks = keep_mask.shape[0]
    reps = 2
    group = NF * tok_dev
    pairs = slots // 2
    shard_ids = jnp.arange(NF + 1, dtype=jnp.int32)
    below = (panel_owner[:, None] < shard_ids[None, :]).astype(jnp.int32)
    first = jnp.sum(below, axis=0)

    smem = pl.BlockSpec(memory_space=pltpu.SMEM)
    vmem = pl.BlockSpec(memory_space=pltpu.VMEM)
    anywhere = pl.BlockSpec(memory_space=pl.ANY)
    dma = lambda n: [pltpu.SemaphoreType.DMA((n,))] * 2
    scale = 1.0 / math.sqrt(group * reps)
    early = 2 * (pairs // 2 + 1)
    late = slots - early
    act_in, grad_in, early_grads, turned, dz_late, kept_row = pl.pallas_call(
        functools.partial(layer_kernel, scale),
        out_shape=(
            jax.ShapeDtypeStruct((NF * slots, tok_dev, bs), BF16),
            jax.ShapeDtypeStruct((tok_dev, width), BF16),
            jax.ShapeDtypeStruct((early, keep, bs, bs), BF16),
            jax.ShapeDtypeStruct((row_blocks, bs, reps * group), BF16),
            jax.ShapeDtypeStruct((reps, late, group, bs), BF16),
            jax.ShapeDtypeStruct((slots * keep,), jnp.int32),
        ),
        in_specs=[smem, smem, vmem, vmem, anywhere],
        out_specs=(vmem, vmem, anywhere, anywhere, anywhere, smem),
        scratch_shapes=[
            pltpu.VMEM((reps, NF, tok_dev, width), BF16),
            pltpu.VMEM((row_blocks, bs, reps * group), BF16),
            pltpu.VMEM((pairs, width, 2 * bs), BF16),
            pltpu.VMEM((slots * keep + 1, bs, bs), BF16),
            pltpu.VMEM((early, keep, bs, bs), BF16),
            pltpu.VMEM((panels, tok_dev, bs), BF16),
            pltpu.VMEM((NF, slots, tok_dev, bs), BF16),
            pltpu.VMEM((NF, slots, tok_dev, bs), BF16),
            pltpu.VMEM((NF, slots, tok_dev, bs), BF16),
            pltpu.VMEM((slots, group, bs), F32),
            pltpu.VMEM((reps, slots, group, bs), BF16),
            pltpu.VMEM((pairs, group, 2 * bs), BF16),
            pltpu.VMEM((NZ, NY, NC, tok_dev, width), BF16),
            pltpu.VMEM((NZ, NY, tok_dev, width), BF16),
            pltpu.VMEM((NZ, tok_dev, width), BF16),
            pltpu.VMEM((NZ, tok_dev, width), BF16),
            pltpu.VMEM((NZ - 1, tok_dev, width), BF16),
            pltpu.VMEM((NZ - 1, tok_dev, width), BF16),
            pltpu.SMEM((slots * row_blocks,), jnp.int32),
            pltpu.SMEM((slots * row_blocks,), jnp.int32),
            pltpu.SemaphoreType.DMA((8,)),
        ]
        + dma(NZ - 1) + dma(NZ) + dma(NZ) + dma(NZ) + dma(4 * NZ) + dma(2 * (NF - 1))
        + dma(2) + dma(2 * (NF - 1)) + dma(4) + dma(4) + dma(4 * (NZ - 1)),
        compiler_params=pltpu.CompilerParams(
            collective_id=0, has_side_effects=True, vmem_limit_bytes=VMEM_LIMIT
        ),
        name="layer",
    )(first, keep_mask, tokens, upstream, blocks.reshape(slots * keep, bs, bs))
    act_out, input_grad, block_grad = pl.pallas_call(
        functools.partial(finish_kernel, scale),
        out_shape=(
            jax.ShapeDtypeStruct((tok_dev, panels * bs), BF16),
            jax.ShapeDtypeStruct((tok_dev, width), BF16),
            jax.ShapeDtypeStruct((slots, keep, bs, bs), BF16),
        ),
        in_specs=[smem, smem, smem, vmem, vmem, anywhere, anywhere, anywhere],
        out_specs=(vmem, vmem, anywhere),
        scratch_shapes=[
            pltpu.VMEM((row_blocks, bs, reps * group), BF16),
            pltpu.VMEM((reps, late, group, bs), BF16),
            pltpu.VMEM((late, keep, bs, bs), BF16),
            pltpu.SemaphoreType.DMA((2 + slots,)),
        ],
        compiler_params=pltpu.CompilerParams(vmem_limit_bytes=VMEM_LIMIT),
        name="finish",
    )(first, panel_owner, kept_row, act_in, grad_in, early_grads, turned, dz_late)
    return (act_out, input_grad, block_grad)


def solution(mesh):
    fits = mesh.shape["rep"] == 2 and mesh.shape["fsdp"] == NF
    return jax.shard_map(
        per_device if fits else per_device_general,
        mesh=mesh,
        in_specs=(
            P(("rep", "fsdp"), None),
            P(("rep", "fsdp"), None),
            P("fsdp", None, None, None),
            P(),
            P(),
        ),
        out_specs=(P(("rep", "fsdp"), None), P(("rep", "fsdp"), None), P("fsdp", None, None, None)),
        check_vma=False,
    )
```

```python
import functools
import math

import jax
import jax.numpy as jnp
from jax import lax
from jax.experimental import pallas as pl
from jax.experimental.pallas import tpu as pltpu
from jax.sharding import PartitionSpec as P

BF16 = jnp.bfloat16
F32 = jnp.float32
MESH = pl.DeviceIdType.MESH
VMEM_LIMIT = 60 * 1024 * 1024
NZ, NY, NC = 4, 2, 2
NF = NZ * NY * NC


def per_device_general(tokens, upstream, blocks, keep_mask, panel_owner):
    shard_count = lax.axis_size("fsdp")
    own_index = lax.axis_index("fsdp")
    tok_dev = tokens.shape[0]
    model_width = tokens.shape[1]
    slot_count = blocks.shape[0]
    keep_count = blocks.shape[1]
    block_size = blocks.shape[3]
    row_blocks = keep_mask.shape[0]
    panel_count = panel_owner.shape[0]
    group_rows = tok_dev * shard_count
    rep_count = lax.axis_size("rep")
    shard_ids = jnp.arange(shard_count, dtype=jnp.int32)
    member = (panel_owner[:, None] == shard_ids[None, :]).astype(jnp.int32)
    counts = jnp.sum(member, axis=0)
    first_panel = jnp.cumsum(counts) - counts
    slot_ids = jnp.arange(slot_count, dtype=jnp.int32)
    panel_table = jnp.clip(first_panel[:, None] + slot_ids[None, :], 0, panel_count - 1)
    is_mine = shard_ids == own_index
    own_first = jnp.sum(jnp.where(is_mine, first_panel, 0))
    own_count = jnp.sum(jnp.where(is_mine, counts, 0))
    own_live = slot_ids < own_count
    own_panels = jnp.clip(own_first + slot_ids, 0, panel_count - 1)
    panel_ids = jnp.arange(panel_count, dtype=jnp.int32)
    panel_pick = (panel_ids[None, :] == own_panels[:, None]).astype(jnp.int32)
    running = jnp.cumsum(keep_mask, axis=0)
    own_running = jnp.sum(panel_pick[:, None, :] * running[None, :, :], axis=2)
    pick_ids = jnp.arange(keep_count, dtype=jnp.int32)
    own_rows = jnp.sum(
        (own_running[:, :, None] <= pick_ids[None, None, :]).astype(jnp.int32), axis=1
    )
    upstream_panels = jnp.transpose(upstream.reshape(tok_dev, panel_count, block_size), (1, 0, 2))
    outgoing = jnp.take(upstream_panels, panel_table.reshape(-1), axis=0)
    incoming = lax.all_to_all(outgoing, "fsdp", split_axis=0, concat_axis=1, tiled=True)
    group_tokens = lax.all_gather(tokens, "fsdp", axis=0, tiled=True)
    all_tokens = lax.all_gather(group_tokens, "rep", axis=0, tiled=True)
    token_blocks = jnp.transpose(all_tokens).reshape(row_blocks, block_size, rep_count * group_rows)

    dense_panels = jnp.zeros((slot_count, row_blocks, block_size, block_size), blocks.dtype)
    dense_panels = dense_panels.at[slot_ids[:, None], own_rows].set(blocks)
    dense = dense_panels.reshape(slot_count, model_width, block_size)
    preact = lax.dot_general(
        group_tokens, dense, (((1,), (1,)), ((), ())), preferred_element_type=jnp.float32
    )
    sigmoid_z = jax.nn.sigmoid(preact)
    activations = (preact * sigmoid_z).astype(jnp.bfloat16)
    slope = sigmoid_z * (1.0 + preact * (1.0 - sigmoid_z))
    cot = jnp.transpose(incoming, (1, 0, 2)).astype(jnp.float32)
    dpre = jnp.where(own_live[None, :, None], cot * slope, 0.0).astype(jnp.bfloat16)
    dpre_all = lax.all_gather(dpre, "rep", axis=0, tiled=True)
    backward = lax.dot_general(
        dpre, dense, (((1, 2), (0, 2)), ((), ())), preferred_element_type=jnp.float32
    )
    input_grad = lax.psum_scatter(
        backward, "fsdp", scatter_dimension=0, tiled=True
    ).astype(jnp.bfloat16)
    returned = lax.all_to_all(activations, "fsdp", split_axis=0, concat_axis=1, tiled=True)
    panel_first = jnp.sum(member * first_panel[None, :], axis=1)
    panel_slot = panel_owner * slot_count + panel_ids - panel_first
    act_panels = jnp.take(returned, panel_slot, axis=1)
    activation_out = act_panels.reshape(tok_dev, panel_count * block_size)
    scale = 1.0 / math.sqrt(group_rows * rep_count)

    def panel_step(nothing, item):
        row_ids, dz = item
        chosen = jnp.take(token_blocks, row_ids, axis=0)
        grad = lax.dot_general(
            chosen, dz, (((2,), (0,)), ((), ())), preferred_element_type=jnp.float32
        )
        return nothing, (grad * scale).astype(jnp.bfloat16)

    nothing, block_grad = lax.scan(
        panel_step, jnp.zeros((), jnp.float32), (own_rows, jnp.transpose(dpre_all, (1, 0, 2)))
    )
    return (activation_out, input_grad, block_grad)


class Place:
    def __init__(self):
        self.rep = lax.axis_index("rep")
        self.me = lax.axis_index("fsdp")
        self.core = self.me % NC
        self.y = (self.me // NC) % NY
        self.z = self.me // (NC * NY)

    def at(self, z, y, core):
        return (z * NY + y) * NC + core

    def z_back(self, step):
        return (self.z + NZ - step) % NZ

    def z_ahead(self, step):
        return (self.z + step) % NZ

    def fsdp_peer(self, step):
        return (self.me + step) % NF

    def greet(self):
        barrier = pltpu.get_barrier_semaphore()
        for step in range(1, NF):
            pl.semaphore_signal(
                barrier, inc=1, device_id=(self.rep, self.fsdp_peer(step)), device_id_type=MESH
            )
        pl.semaphore_signal(barrier, inc=1, device_id=(1 - self.rep, self.me), device_id_type=MESH)
        pl.semaphore_wait(barrier, NF)


def transfer(src, dst, send_sem, recv_sem, device):
    return pltpu.make_async_remote_copy(
        src_ref=src,
        dst_ref=dst,
        send_sem=send_sem,
        recv_sem=recv_sem,
        device_id=device,
        device_id_type=MESH,
    )


def send(src, dst, sems, slot, device):
    send_sems, recv_sems = sems
    copy = pltpu.make_async_remote_copy(
        src_ref=src,
        dst_ref=dst,
        send_sem=send_sems.at[slot],
        recv_sem=recv_sems.at[slot],
        device_id=device,
        device_id_type=MESH,
    )
    copy.start()
    return copy


def layer_kernel(
    scale,
    first, keep, tokens, upstream, blocks_hbm,
    act_in, grad_out, early_grads, turned_out, dz_late, kept_row,
    all_tokens, turned, dense, blocks, grads, up3, outgoing, incoming,
    act, slope, dz_both, dz_flat, part, r1, s2, r2, s3, r3, grad_sum, run, place_of,
    local, z_s, z_r, y_s, y_r, x_s, x_r, d_s, d_r, c_s, c_r, u_s, u_r,
    v_s, v_r, a_s, a_r, p_s, p_r, q_s, q_r, t_s, t_r,
):
    place = Place()
    rep, me, z, y, core = place.rep, place.me, place.z, place.y, place.core
    slots, bs = outgoing.shape[1], outgoing.shape[3]
    row_blocks, panels = keep.shape
    kept = early_grads.shape[1]
    tok_dev, width = tokens.shape
    rows = NF * tok_dev
    pairs = slots // 2
    y_peer = (rep, place.at(z, 1 - y, core))
    x_peer = (1 - rep, me)
    core_peer = (rep, place.at(z, y, 1 - core))
    y_sems, x_sems = (y_s, y_r), (x_s, x_r)
    d_sems, c_sems, u_sems = (d_s, d_r), (c_s, c_r), (u_s, u_r)
    early = pairs // 2 + 1
    halves = ((0, 2 * early), (2 * early, slots - 2 * early))

    load_blocks = pltpu.make_async_copy(
        blocks_hbm, blocks.at[pl.ds(0, slots * kept)], local.at[0]
    )
    load_blocks.start()
    all_tokens[rep, me] = tokens[...]
    place.greet()

    steps = (
        0,
        jnp.where(z == 0, 3, 1),
        jnp.where((z == 0) | (z == NZ - 1), 2, 3),
        jnp.where(z == 0, 1, jnp.where(z == NZ - 1, 3, 2)),
    )
    up_peer = (rep, place.at(place.z_ahead(1), y, core))
    down_peer = (rep, place.at(place.z_back(1), y, core))

    def line_piece(n):
        return all_tokens.at[rep, place.at(place.z_back(steps[n]), y, core)]

    def line_up(n):
        piece = line_piece(n)
        return transfer(piece, piece, z_s.at[n], z_r.at[steps[n]], up_peer)

    def line_down(n):
        piece = line_piece(n)
        slot = 2 if n == 0 else jnp.maximum(steps[n] - 2, 0)
        return transfer(piece, piece, z_s.at[NZ + n], z_r.at[slot], down_peer)

    def goes_up(n):
        return z < NZ - 1 if n == 0 else (z >= steps[n]) & (z < NZ - 1)

    def goes_down(n):
        return z > 0 if n == 0 else (z < steps[n]) & (z > 0)

    def pass_on(n):
        @pl.when(goes_up(n))
        def _():
            line_up(n).start()

        @pl.when(goes_down(n))
        def _():
            line_down(n).start()

    y_copies, x_copies, d_copies, c_copies = [], [], [None] * NZ, [None] * (4 * NZ)

    def spread(n):
        piece = line_piece(n)
        y_copies.append(send(piece, piece, y_sems, n, y_peer))
        x_copies.append(send(piece, piece, x_sems, n, x_peer))
        c_copies[n] = send(piece, piece, c_sems, n, core_peer)

    pass_on(0)
    spread(0)

    for c in range(panels):
        up3[c] = upstream[:, c * bs:(c + 1) * bs]
    u_copies = [[], []]
    for half, (start, size) in enumerate(halves):
        @pl.loop(0, NF)
        def _(k):
            for p in range(start, start + size):
                outgoing[k, p] = up3[jnp.minimum(first[k] + p, panels - 1)]

        for step in range(1, NF):
            peer = place.fsdp_peer(step)
            span = pl.ds(start, size)
            u_copies[half].append(send(
                outgoing.at[peer, span], incoming.at[me, span], u_sems,
                half * (NF - 1) + step - 1, (rep, peer),
            ))
    incoming[me] = outgoing[me]

    @pl.loop(0, slots)
    def _(p):
        c = jnp.minimum(first[me] + p, panels - 1)
        count = jnp.int32(0)
        for r in range(row_blocks):
            bit = keep[r, c]
            count = count + bit
            run[p * row_blocks + r] = count
            place_of[p * row_blocks + r] = jnp.where(
                bit == 1, p * kept + jnp.clip(count - 1, 0, kept - 1), slots * kept
            )

    blocks[slots * kept] = jnp.zeros((bs, bs), BF16)
    load_blocks.wait()

    def build(start, stop):
        @pl.loop(start, stop)
        def _(i):
            for side in range(2):
                for r in range(row_blocks):
                    at = place_of[(2 * i + side) * row_blocks + r]
                    dense[i, r * bs:(r + 1) * bs, side * bs:(side + 1) * bs] = blocks[at]

    for n in range(1, NZ):
        piece = line_piece(n)
        transfer(piece, piece, z_s.at[n], z_r.at[steps[n] - 1], up_peer).wait_recv()
        pass_on(n)
        spread(n)
        build(n - 1, n)
    for n in range(NZ):
        f_x = place.at(place.z_back(steps[n]), y, core)
        f_y = place.at(place.z_back(steps[n]), 1 - y, core)
        y_copies[n].wait_recv()
        piece = all_tokens.at[rep, f_y]
        c_copies[2 * NZ + n] = send(piece, piece, c_sems, 2 * NZ + n, core_peer)
        d_copies[n] = send(piece, piece, d_sems, n, x_peer)
        x_copies[n].wait_recv()
        piece = all_tokens.at[1 - rep, f_x]
        c_copies[NZ + n] = send(piece, piece, c_sems, NZ + n, core_peer)
        build(NZ - 1 + n, NZ + n)

    @pl.loop(0, slots)
    def _(p):
        @pl.loop(0, kept)
        def _(j):
            row = jnp.int32(0)
            for r in range(row_blocks):
                row = row + jnp.where(run[p * row_blocks + r] <= j, 1, 0)
            kept_row[p * kept + j] = jnp.minimum(row, row_blocks - 1)

    for step in range(NZ):
        c_copies[step].wait_recv()
        c_copies[2 * NZ + step].wait_recv()

    count = first[me + 1] - first[me]
    v_copies, a_copies = [], []
    for half, (start, size) in enumerate(halves):
        @pl.loop(start // 2, (start + size) // 2)
        def _(i):
            preact = jnp.dot(
                all_tokens[rep].reshape(rows, width), dense[i], preferred_element_type=F32
            )
            for side in range(2):
                slot = 2 * i + side
                zed = preact[:, side * bs:(side + 1) * bs]
                sig = jax.nn.sigmoid(zed)
                act[:, slot] = (zed * sig).astype(BF16).reshape(NF, tok_dev, bs)
                slope[slot] = sig * (1.0 + zed * (1.0 - sig))

        span = pl.ds(start, size)
        for step in range(1, NF):
            peer = place.fsdp_peer(step)
            a_copies.append(send(
                act.at[peer, span], act_in.at[pl.ds(me * slots + start, size)], (a_s, a_r),
                half * (NF - 1) + step - 1, (rep, peer),
            ))
        if half == 0:
            for step in range(NZ):
                d_copies[step].wait_recv()
                piece = all_tokens.at[
                    1 - rep, place.at(place.z_back(steps[step]), 1 - y, core)
                ]
                c_copies[3 * NZ + step] = send(piece, piece, c_sems, 3 * NZ + step, core_peer)
    act_in[pl.ds(me * slots, slots)] = act[me]

    def turn(group):
        @pl.loop(0, row_blocks)
        def _(r):
            lanes = pl.ds(pl.multiple_of(r * bs, bs), bs)
            span = pl.ds(pl.multiple_of(group * rows, rows), rows)
            turned[r, :, span] = all_tokens[group, :, :, lanes].reshape(rows, bs).T

    turn(rep)
    for half, (start, size) in enumerate(halves):
        for copy in u_copies[half]:
            copy.wait_recv()

        @pl.loop(start // 2, (start + size) // 2)
        def _(i):
            for side in range(2):
                slot = 2 * i + side
                cot = incoming[:, slot].reshape(rows, bs).astype(F32)
                value = jnp.where(slot < count, cot * slope[slot], 0.0).astype(BF16)
                dz_both[rep, slot] = value
                dz_flat[i, :, side * bs:(side + 1) * bs] = value

        piece = dz_both.at[rep, pl.ds(start, size)]
        v_copies.append(send(piece, piece, (v_s, v_r), half, x_peer))

    chunks = 4
    chunk = width // chunks
    p_copies, q_copies = [], []
    for n in range(chunks):
        span = pl.ds(n * chunk, chunk)
        total = jnp.zeros((rows, chunk), F32)
        for i in range(pairs):
            total = total + lax.dot_general(
                dz_flat[i], dense[i, span, :], (((1,), (1,)), ((), ())),
                preferred_element_type=F32,
            )
        part[:, :, :, :, span] = total.astype(BF16).reshape(NZ, NY, NC, tok_dev, chunk)
        p_copies.append(send(
            part.at[:, :, 1 - core, :, span], r1.at[:, :, :, span], (p_s, p_r), n, core_peer
        ))
    for n in range(chunks):
        span = pl.ds(n * chunk, chunk)
        p_copies[n].wait_recv()
        s2[:, :, span] = (
            part[:, 1 - y, core, :, span].astype(F32) + r1[:, 1 - y, :, span].astype(F32)
        ).astype(BF16)
        q_copies.append(send(s2.at[:, :, span], r2.at[:, :, span], (q_s, q_r), n, y_peer))

    def column_sum(at_z, span):
        return (
            part[at_z, y, core, :, span].astype(F32)
            + r1[at_z, y, :, span].astype(F32)
            + r2[at_z, :, span].astype(F32)
        )

    def line_sum(n, e, up):
        span = pl.ds(n * chunk, chunk)
        way = 0 if up else 1
        at = (way * chunks + n) * NZ + e
        return transfer(
            s3.at[way, e, :, span], r3.at[way, e - 1, :, span], t_s.at[at], t_r.at[at - 1],
            up_peer if up else down_peer,
        )

    def line_arrival(n, e, up):
        span = pl.ds(n * chunk, chunk)
        way = 0 if up else 1
        at = (way * chunks + n) * NZ + e
        return transfer(
            s3.at[way, e, :, span], r3.at[way, e, :, span], t_s.at[at], t_r.at[at],
            up_peer if up else down_peer,
        )

    def ways():
        for up in (True, False):
            way = 0 if up else 1
            has_source = z > 0 if up else z < NZ - 1
            yield up, way, has_source

    def reaches(e, up):
        return z + e < NZ if up else z >= e

    def to_z(n):
        span = pl.ds(n * chunk, chunk)
        q_copies[n].wait_recv()
        for e in range(NZ - 1, 0, -1):
            for up, way, has_source in ways():
                target = z + e if up else z - e

                @pl.when(reaches(e, up) & has_source)
                def _():
                    line_arrival(n, e, up).wait_recv()
                    total = column_sum(target, span) + r3[way, e, :, span].astype(F32)
                    s3[way, e, :, span] = total.astype(BF16)

                @pl.when(reaches(e, up) & ~has_source)
                def _():
                    s3[way, e, :, span] = column_sum(target, span).astype(BF16)

                @pl.when(reaches(e, up))
                def _():
                    line_sum(n, e, up).start()

    stores = []

    def store(src, dst):
        copy = pltpu.make_async_copy(src, dst, local.at[1 + len(stores)])
        copy.start()
        stores.append(copy)

    def weight(start, size):
        @pl.loop(start, start + size)
        def _(p):
            weight_panel(scale, kept_row, p * kept, turned, dz_both[:, p], grads, p)

        span = pl.ds(start, size)
        store(grads.at[span], early_grads.at[span])

    for step in range(NZ):
        c_copies[NZ + step].wait_recv()
        c_copies[3 * NZ + step].wait_recv()
    turn(1 - rep)
    store(turned, turned_out)
    to_z(0)
    to_z(1)
    v_copies[0].wait_recv()
    cut = halves[0][1] // 2
    weight(0, cut)
    to_z(2)
    to_z(3)
    weight(cut, halves[0][1] - cut)
    v_copies[1].wait_recv()
    store(dz_both.at[:, pl.ds(*halves[1])], dz_late)
    for n in range(chunks):
        span = pl.ds(n * chunk, chunk)
        grad_sum[:, span] = column_sum(z, span)
        for up, way, has_source in ways():
            @pl.when(has_source)
            def _():
                line_arrival(n, 0, up).wait_recv()
                grad_sum[:, span] += r3[way, 0, :, span].astype(F32)

        grad_out[:, span] = grad_sum[:, span].astype(BF16)
    for copy in a_copies:
        copy.wait_recv()
    for copy in stores:
        copy.wait()
    sent = y_copies + x_copies + d_copies + c_copies + u_copies[0]
    sent += u_copies[1] + v_copies + a_copies + p_copies + q_copies
    for copy in sent:
        copy.wait_send()
    for n in range(NZ):
        @pl.when(goes_up(n))
        def _():
            line_up(n).wait_send()

        @pl.when(goes_down(n))
        def _():
            line_down(n).wait_send()

    for n in range(chunks):
        for e in range(1, NZ):
            for up, way, has_source in ways():
                @pl.when(reaches(e, up))
                def _():
                    line_sum(n, e, up).wait_send()


def weight_panel(scale, kept_row, base, turned, dz, out, at):
    bs = dz.shape[-1]
    value = dz.reshape(-1, bs)
    for j in range(0, out.shape[1], 4):
        chosen = jnp.concatenate([turned[kept_row[base + j + t]] for t in range(4)], axis=0)
        grad = jnp.dot(chosen, value, preferred_element_type=F32) * scale
        out[at, j:j + 4] = grad.astype(BF16).reshape(4, bs, bs)


def finish_kernel(
    scale,
    first, owner, kept_row, act_in, grad_in, early_grads, turned_hbm, dz_hbm,
    act_out, grad_out, block_grad,
    turned, dz, grads, sems,
):
    early, kept = early_grads.shape[:2]
    slots = grads.shape[0]
    late = slots - early
    bs = turned.shape[1]
    panels = act_out.shape[1] // bs
    loads = [
        pltpu.make_async_copy(dz_hbm, dz, sems.at[0]),
        pltpu.make_async_copy(turned_hbm, turned, sems.at[1]),
        pltpu.make_async_copy(early_grads, grads.at[pl.ds(0, early)], sems.at[2]),
    ]
    for copy in loads:
        copy.start()
    grad_out[...] = grad_in[...]

    @pl.loop(0, panels)
    def _(c):
        k = owner[c]
        at = jnp.clip(k * slots + c - first[k], 0, NF * slots - 1)
        act_out[:, pl.ds(pl.multiple_of(c * bs, bs), bs)] = act_in[at]

    for copy in loads:
        copy.wait()
    span = pl.ds(0, early)
    stores = [pltpu.make_async_copy(grads.at[span], block_grad.at[span], sems.at[3])]
    stores[0].start()
    for s in range(late):
        slot = early + s
        weight_panel(scale, kept_row, slot * kept, turned, dz[:, s], grads, slot)
        stores.append(
            pltpu.make_async_copy(grads.at[slot], block_grad.at[slot], sems.at[4 + s])
        )
        stores[-1].start()
    for copy in stores:
        copy.wait()


def per_device(tokens, upstream, blocks, keep_mask, panel_owner):
    tok_dev, width = tokens.shape
    slots, keep, bs, _ = blocks.shape
    panels = panel_owner.shape[0]
    row_blocks = keep_mask.shape[0]
    reps = 2
    group = NF * tok_dev
    pairs = slots // 2
    shard_ids = jnp.arange(NF + 1, dtype=jnp.int32)
    below = (panel_owner[:, None] < shard_ids[None, :]).astype(jnp.int32)
    first = jnp.sum(below, axis=0)

    smem = pl.BlockSpec(memory_space=pltpu.SMEM)
    vmem = pl.BlockSpec(memory_space=pltpu.VMEM)
    anywhere = pl.BlockSpec(memory_space=pl.ANY)
    dma = lambda n: [pltpu.SemaphoreType.DMA((n,))] * 2
    scale = 1.0 / math.sqrt(group * reps)
    early = 2 * (pairs // 2 + 1)
    late = slots - early
    act_in, grad_in, early_grads, turned, dz_late, kept_row = pl.pallas_call(
        functools.partial(layer_kernel, scale),
        out_shape=(
            jax.ShapeDtypeStruct((NF * slots, tok_dev, bs), BF16),
            jax.ShapeDtypeStruct((tok_dev, width), BF16),
            jax.ShapeDtypeStruct((early, keep, bs, bs), BF16),
            jax.ShapeDtypeStruct((row_blocks, bs, reps * group), BF16),
            jax.ShapeDtypeStruct((reps, late, group, bs), BF16),
            jax.ShapeDtypeStruct((slots * keep,), jnp.int32),
        ),
        in_specs=[smem, smem, vmem, vmem, anywhere],
        out_specs=(vmem, vmem, anywhere, anywhere, anywhere, smem),
        scratch_shapes=[
            pltpu.VMEM((reps, NF, tok_dev, width), BF16),
            pltpu.VMEM((row_blocks, bs, reps * group), BF16),
            pltpu.VMEM((pairs, width, 2 * bs), BF16),
            pltpu.VMEM((slots * keep + 1, bs, bs), BF16),
            pltpu.VMEM((early, keep, bs, bs), BF16),
            pltpu.VMEM((panels, tok_dev, bs), BF16),
            pltpu.VMEM((NF, slots, tok_dev, bs), BF16),
            pltpu.VMEM((NF, slots, tok_dev, bs), BF16),
            pltpu.VMEM((NF, slots, tok_dev, bs), BF16),
            pltpu.VMEM((slots, group, bs), F32),
            pltpu.VMEM((reps, slots, group, bs), BF16),
            pltpu.VMEM((pairs, group, 2 * bs), BF16),
            pltpu.VMEM((NZ, NY, NC, tok_dev, width), BF16),
            pltpu.VMEM((NZ, NY, tok_dev, width), BF16),
            pltpu.VMEM((NZ, tok_dev, width), BF16),
            pltpu.VMEM((NZ, tok_dev, width), BF16),
            pltpu.VMEM((2, NZ, tok_dev, width), BF16),
            pltpu.VMEM((2, NZ, tok_dev, width), BF16),
            pltpu.VMEM((tok_dev, width), F32),
            pltpu.SMEM((slots * row_blocks,), jnp.int32),
            pltpu.SMEM((slots * row_blocks,), jnp.int32),
            pltpu.SemaphoreType.DMA((8,)),
        ]
        + dma(2 * NZ) + dma(NZ) + dma(NZ) + dma(NZ) + dma(4 * NZ) + dma(2 * (NF - 1))
        + dma(2) + dma(2 * (NF - 1)) + dma(4) + dma(4) + dma(2 * 4 * NZ),
        compiler_params=pltpu.CompilerParams(
            collective_id=0, has_side_effects=True, vmem_limit_bytes=VMEM_LIMIT
        ),
        name="layer",
    )(first, keep_mask, tokens, upstream, blocks.reshape(slots * keep, bs, bs))
    act_out, input_grad, block_grad = pl.pallas_call(
        functools.partial(finish_kernel, scale),
        out_shape=(
            jax.ShapeDtypeStruct((tok_dev, panels * bs), BF16),
            jax.ShapeDtypeStruct((tok_dev, width), BF16),
            jax.ShapeDtypeStruct((slots, keep, bs, bs), BF16),
        ),
        in_specs=[smem, smem, smem, vmem, vmem, anywhere, anywhere, anywhere],
        out_specs=(vmem, vmem, anywhere),
        scratch_shapes=[
            pltpu.VMEM((row_blocks, bs, reps * group), BF16),
            pltpu.VMEM((reps, late, group, bs), BF16),
            pltpu.VMEM((slots, keep, bs, bs), BF16),
            pltpu.SemaphoreType.DMA((4 + late,)),
        ],
        compiler_params=pltpu.CompilerParams(vmem_limit_bytes=VMEM_LIMIT),
        name="finish",
    )(first, panel_owner, kept_row, act_in, grad_in, early_grads, turned, dz_late)
    return (act_out, input_grad, block_grad)


def solution(mesh):
    fits = mesh.shape["rep"] == 2 and mesh.shape["fsdp"] == NF
    return jax.shard_map(
        per_device if fits else per_device_general,
        mesh=mesh,
        in_specs=(
            P(("rep", "fsdp"), None),
            P(("rep", "fsdp"), None),
            P("fsdp", None, None, None),
            P(),
            P(),
        ),
        out_specs=(P(("rep", "fsdp"), None), P(("rep", "fsdp"), None), P("fsdp", None, None, None)),
        check_vma=False,
    )
```

```python
import functools
import math

import jax
import jax.numpy as jnp
from jax import lax
from jax.experimental import pallas as pl
from jax.experimental.pallas import tpu as pltpu
from jax.sharding import PartitionSpec as P

BF16 = jnp.bfloat16
F32 = jnp.float32
MESH = pl.DeviceIdType.MESH
VMEM_LIMIT = 60 * 1024 * 1024
NZ, NY, NC = 4, 2, 2
NF = NZ * NY * NC


def per_device_general(tokens, upstream, blocks, keep_mask, panel_owner):
    shard_count = lax.axis_size("fsdp")
    own_index = lax.axis_index("fsdp")
    tok_dev = tokens.shape[0]
    model_width = tokens.shape[1]
    slot_count = blocks.shape[0]
    keep_count = blocks.shape[1]
    block_size = blocks.shape[3]
    row_blocks = keep_mask.shape[0]
    panel_count = panel_owner.shape[0]
    group_rows = tok_dev * shard_count
    rep_count = lax.axis_size("rep")
    shard_ids = jnp.arange(shard_count, dtype=jnp.int32)
    member = (panel_owner[:, None] == shard_ids[None, :]).astype(jnp.int32)
    counts = jnp.sum(member, axis=0)
    first_panel = jnp.cumsum(counts) - counts
    slot_ids = jnp.arange(slot_count, dtype=jnp.int32)
    panel_table = jnp.clip(first_panel[:, None] + slot_ids[None, :], 0, panel_count - 1)
    is_mine = shard_ids == own_index
    own_first = jnp.sum(jnp.where(is_mine, first_panel, 0))
    own_count = jnp.sum(jnp.where(is_mine, counts, 0))
    own_live = slot_ids < own_count
    own_panels = jnp.clip(own_first + slot_ids, 0, panel_count - 1)
    panel_ids = jnp.arange(panel_count, dtype=jnp.int32)
    panel_pick = (panel_ids[None, :] == own_panels[:, None]).astype(jnp.int32)
    running = jnp.cumsum(keep_mask, axis=0)
    own_running = jnp.sum(panel_pick[:, None, :] * running[None, :, :], axis=2)
    pick_ids = jnp.arange(keep_count, dtype=jnp.int32)
    own_rows = jnp.sum(
        (own_running[:, :, None] <= pick_ids[None, None, :]).astype(jnp.int32), axis=1
    )
    upstream_panels = jnp.transpose(upstream.reshape(tok_dev, panel_count, block_size), (1, 0, 2))
    outgoing = jnp.take(upstream_panels, panel_table.reshape(-1), axis=0)
    incoming = lax.all_to_all(outgoing, "fsdp", split_axis=0, concat_axis=1, tiled=True)
    group_tokens = lax.all_gather(tokens, "fsdp", axis=0, tiled=True)
    all_tokens = lax.all_gather(group_tokens, "rep", axis=0, tiled=True)
    token_blocks = jnp.transpose(all_tokens).reshape(row_blocks, block_size, rep_count * group_rows)

    dense_panels = jnp.zeros((slot_count, row_blocks, block_size, block_size), blocks.dtype)
    dense_panels = dense_panels.at[slot_ids[:, None], own_rows].set(blocks)
    dense = dense_panels.reshape(slot_count, model_width, block_size)
    preact = lax.dot_general(
        group_tokens, dense, (((1,), (1,)), ((), ())), preferred_element_type=jnp.float32
    )
    sigmoid_z = jax.nn.sigmoid(preact)
    activations = (preact * sigmoid_z).astype(jnp.bfloat16)
    slope = sigmoid_z * (1.0 + preact * (1.0 - sigmoid_z))
    cot = jnp.transpose(incoming, (1, 0, 2)).astype(jnp.float32)
    dpre = jnp.where(own_live[None, :, None], cot * slope, 0.0).astype(jnp.bfloat16)
    dpre_all = lax.all_gather(dpre, "rep", axis=0, tiled=True)
    backward = lax.dot_general(
        dpre, dense, (((1, 2), (0, 2)), ((), ())), preferred_element_type=jnp.float32
    )
    input_grad = lax.psum_scatter(
        backward, "fsdp", scatter_dimension=0, tiled=True
    ).astype(jnp.bfloat16)
    returned = lax.all_to_all(activations, "fsdp", split_axis=0, concat_axis=1, tiled=True)
    panel_first = jnp.sum(member * first_panel[None, :], axis=1)
    panel_slot = panel_owner * slot_count + panel_ids - panel_first
    act_panels = jnp.take(returned, panel_slot, axis=1)
    activation_out = act_panels.reshape(tok_dev, panel_count * block_size)
    scale = 1.0 / math.sqrt(group_rows * rep_count)

    def panel_step(nothing, item):
        row_ids, dz = item
        chosen = jnp.take(token_blocks, row_ids, axis=0)
        grad = lax.dot_general(
            chosen, dz, (((2,), (0,)), ((), ())), preferred_element_type=jnp.float32
        )
        return nothing, (grad * scale).astype(jnp.bfloat16)

    nothing, block_grad = lax.scan(
        panel_step, jnp.zeros((), jnp.float32), (own_rows, jnp.transpose(dpre_all, (1, 0, 2)))
    )
    return (activation_out, input_grad, block_grad)


class Place:
    def __init__(self):
        self.rep = lax.axis_index("rep")
        self.me = lax.axis_index("fsdp")
        self.core = self.me % NC
        self.y = (self.me // NC) % NY
        self.z = self.me // (NC * NY)

    def at(self, z, y, core):
        return (z * NY + y) * NC + core

    def z_back(self, step):
        return (self.z + NZ - step) % NZ

    def z_ahead(self, step):
        return (self.z + step) % NZ

    def fsdp_peer(self, step):
        return (self.me + step) % NF

    def greet(self):
        barrier = pltpu.get_barrier_semaphore()
        for step in range(1, NF):
            pl.semaphore_signal(
                barrier, inc=1, device_id=(self.rep, self.fsdp_peer(step)), device_id_type=MESH
            )
        pl.semaphore_signal(barrier, inc=1, device_id=(1 - self.rep, self.me), device_id_type=MESH)
        pl.semaphore_wait(barrier, NF)


def send(src, dst, sems, slot, device):
    send_sems, recv_sems = sems
    copy = pltpu.make_async_remote_copy(
        src_ref=src,
        dst_ref=dst,
        send_sem=send_sems.at[slot],
        recv_sem=recv_sems.at[slot],
        device_id=device,
        device_id_type=MESH,
    )
    copy.start()
    return copy


def layer_kernel(
    scale,
    first, keep, tokens, upstream, blocks_hbm,
    act_in, grad_out, grads_out,
    all_tokens, turned, dense, blocks, grads, up3, outgoing, incoming,
    act, slope, dz_both, dz_flat, part, r1, s2, r2, s3, r3, run, place_of, kept_row,
    local, z_s, z_r, y_s, y_r, x_s, x_r, d_s, d_r, c_s, c_r, u_s, u_r,
    v_s, v_r, a_s, a_r, p_s, p_r, q_s, q_r, t_s, t_r,
):
    place = Place()
    rep, me, z, y, core = place.rep, place.me, place.z, place.y, place.core
    slots, bs = outgoing.shape[1], outgoing.shape[3]
    row_blocks, panels = keep.shape
    kept = grads_out.shape[1]
    tok_dev, width = tokens.shape
    rows = NF * tok_dev
    pairs = slots // 2
    y_peer = (rep, place.at(z, 1 - y, core))
    x_peer = (1 - rep, me)
    core_peer = (rep, place.at(z, y, 1 - core))
    z_sems, y_sems, x_sems = (z_s, z_r), (y_s, y_r), (x_s, x_r)
    d_sems, c_sems, u_sems = (d_s, d_r), (c_s, c_r), (u_s, u_r)
    early = pairs // 2 + 1
    halves = ((0, 2 * early), (2 * early, slots - 2 * early))

    load_blocks = pltpu.make_async_copy(
        blocks_hbm, blocks.at[pl.ds(0, slots * kept)], local.at[0]
    )
    load_blocks.start()
    all_tokens[rep, me] = tokens[...]
    place.greet()

    own = all_tokens.at[rep, me]
    z_copies = {}
    for step in range(1, NZ):
        peer = (rep, place.at(place.z_ahead(step), y, core))
        z_copies[step] = send(own, own, z_sems, step - 1, peer)
    y_copies, x_copies, d_copies, c_copies = [], [], [None] * NZ, [None] * (4 * NZ)

    def spread(step):
        piece = all_tokens.at[rep, place.at(place.z_back(step), y, core)]
        y_copies.append(send(piece, piece, y_sems, step, y_peer))
        x_copies.append(send(piece, piece, x_sems, step, x_peer))
        c_copies[step] = send(piece, piece, c_sems, step, core_peer)

    spread(0)

    for c in range(panels):
        up3[c] = upstream[:, c * bs:(c + 1) * bs]
    u_copies = [[], []]

    def send_cotangents(half):
        start, size = halves[half]

        @pl.loop(0, NF)
        def _(k):
            for p in range(start, start + size):
                outgoing[k, p] = up3[jnp.minimum(first[k] + p, panels - 1)]

        span = pl.ds(start, size)
        incoming[me, span] = outgoing[me, span]
        for step in range(1, NF):
            peer = place.fsdp_peer(step)
            u_copies[half].append(send(
                outgoing.at[peer, span], incoming.at[me, span], u_sems,
                half * (NF - 1) + step - 1, (rep, peer),
            ))

    send_cotangents(0)

    @pl.loop(0, slots)
    def _(p):
        c = jnp.minimum(first[me] + p, panels - 1)
        count = jnp.int32(0)
        for r in range(row_blocks):
            bit = keep[r, c]
            count = count + bit
            run[p * row_blocks + r] = count
            place_of[p * row_blocks + r] = jnp.where(
                bit == 1, p * kept + jnp.clip(count - 1, 0, kept - 1), slots * kept
            )

    blocks[slots * kept] = jnp.zeros((bs, bs), BF16)
    load_blocks.wait()

    def build(start, stop):
        @pl.loop(start, stop)
        def _(i):
            for side in range(2):
                for r in range(row_blocks):
                    at = place_of[(2 * i + side) * row_blocks + r]
                    dense[i, r * bs:(r + 1) * bs, side * bs:(side + 1) * bs] = blocks[at]

    for step in range(1, NZ):
        z_copies[step].wait_recv()
        spread(step)
        build(step - 1, step)
    send_cotangents(1)
    for step in range(NZ):
        f_x = place.at(place.z_back(step), y, core)
        f_y = place.at(place.z_back(step), 1 - y, core)
        y_copies[step].wait_recv()
        piece = all_tokens.at[rep, f_y]
        c_copies[2 * NZ + step] = send(piece, piece, c_sems, 2 * NZ + step, core_peer)
        d_copies[step] = send(piece, piece, d_sems, step, x_peer)
        x_copies[step].wait_recv()
        piece = all_tokens.at[1 - rep, f_x]
        c_copies[NZ + step] = send(piece, piece, c_sems, NZ + step, core_peer)
        build(NZ - 1 + step, NZ + step)

    @pl.loop(0, slots)
    def _(p):
        @pl.loop(0, kept)
        def _(j):
            row = jnp.int32(0)
            for r in range(row_blocks):
                row = row + jnp.where(run[p * row_blocks + r] <= j, 1, 0)
            kept_row[p * kept + j] = jnp.minimum(row, row_blocks - 1)

    for step in range(NZ):
        c_copies[step].wait_recv()
        c_copies[2 * NZ + step].wait_recv()

    count = first[me + 1] - first[me]
    v_copies, a_copies = [], []
    for half, (start, size) in enumerate(halves):
        @pl.loop(start // 2, (start + size) // 2)
        def _(i):
            preact = jnp.dot(
                all_tokens[rep].reshape(rows, width), dense[i], preferred_element_type=F32
            )
            for side in range(2):
                slot = 2 * i + side
                zed = preact[:, side * bs:(side + 1) * bs]
                sig = jax.nn.sigmoid(zed)
                act[:, slot] = (zed * sig).astype(BF16).reshape(NF, tok_dev, bs)
                slope[slot] = sig * (1.0 + zed * (1.0 - sig))

        if half == 0:
            for step in range(NZ):
                d_copies[step].wait_recv()
                piece = all_tokens.at[1 - rep, place.at(place.z_back(step), 1 - y, core)]
                c_copies[3 * NZ + step] = send(piece, piece, c_sems, 3 * NZ + step, core_peer)
    act_in[pl.ds(me * slots, slots)] = act[me]

    def send_activations(half):
        start, size = halves[half]
        for step in range(1, NF):
            peer = place.fsdp_peer(step)
            a_copies.append(send(
                act.at[peer, pl.ds(start, size)], act_in.at[pl.ds(me * slots + start, size)],
                (a_s, a_r), half * (NF - 1) + step - 1, (rep, peer),
            ))

    def turn(group):
        @pl.loop(0, row_blocks)
        def _(r):
            lanes = pl.ds(pl.multiple_of(r * bs, bs), bs)
            span = pl.ds(pl.multiple_of(group * rows, rows), rows)
            turned[r, :, span] = all_tokens[group, :, :, lanes].reshape(rows, bs).T

    turn(rep)
    for half, (start, size) in enumerate(halves):
        for copy in u_copies[half]:
            copy.wait_recv()

        @pl.loop(start // 2, (start + size) // 2)
        def _(i):
            for side in range(2):
                slot = 2 * i + side
                cot = incoming[:, slot].reshape(rows, bs).astype(F32)
                value = jnp.where(slot < count, cot * slope[slot], 0.0).astype(BF16)
                dz_both[rep, slot] = value
                dz_flat[i, :, side * bs:(side + 1) * bs] = value

        piece = dz_both.at[rep, pl.ds(start, size)]
        v_copies.append(send(piece, piece, (v_s, v_r), half, x_peer))
        if half == 0:
            send_activations(0)

    chunks = 4
    chunk = width // chunks
    p_copies, q_copies, t_copies = [], [], []
    for n in range(chunks):
        span = pl.ds(n * chunk, chunk)
        total = jnp.zeros((rows, chunk), F32)
        for i in range(pairs):
            total = total + lax.dot_general(
                dz_flat[i], dense[i, span, :], (((1,), (1,)), ((), ())),
                preferred_element_type=F32,
            )
        part[:, :, :, :, span] = total.astype(BF16).reshape(NZ, NY, NC, tok_dev, chunk)
        p_copies.append(send(
            part.at[:, :, 1 - core, :, span], r1.at[:, :, :, span], (p_s, p_r), n, core_peer
        ))
    for n in range(chunks):
        span = pl.ds(n * chunk, chunk)
        p_copies[n].wait_recv()
        s2[:, :, span] = (
            part[:, 1 - y, core, :, span].astype(F32) + r1[:, 1 - y, :, span].astype(F32)
        ).astype(BF16)
        q_copies.append(send(s2.at[:, :, span], r2.at[:, :, span], (q_s, q_r), n, y_peer))
    send_activations(1)

    def column_sum(at_z, span):
        return (
            part[at_z, y, core, :, span].astype(F32)
            + r1[at_z, y, :, span].astype(F32)
            + r2[at_z, :, span].astype(F32)
        )

    def to_z(n):
        span = pl.ds(n * chunk, chunk)
        q_copies[n].wait_recv()
        for step in range(1, NZ):
            s3[step - 1, :, span] = column_sum(place.z_ahead(step), span).astype(BF16)
            peer = (rep, place.at(place.z_ahead(step), y, core))
            t_copies.append(send(
                s3.at[step - 1, :, span], r3.at[step - 1, :, span], (t_s, t_r),
                n * (NZ - 1) + step - 1, peer,
            ))

    stores = []

    def store(src, dst):
        copy = pltpu.make_async_copy(src, dst, local.at[1 + len(stores)])
        copy.start()
        stores.append(copy)

    def weight(start, size):
        @pl.loop(start, start + size)
        def _(p):
            weight_panel(scale, kept_row, p * kept, turned, dz_both[:, p], grads, p)

        span = pl.ds(start, size)
        store(grads.at[span], grads_out.at[span])

    for step in range(NZ):
        c_copies[NZ + step].wait_recv()
        c_copies[3 * NZ + step].wait_recv()
    turn(1 - rep)
    to_z(0)
    to_z(1)
    v_copies[0].wait_recv()
    cut = halves[0][1] // 2
    weight(0, cut)
    to_z(2)
    to_z(3)
    weight(cut, halves[0][1] - cut)
    v_copies[1].wait_recv()
    weight(*halves[1])
    for n in range(chunks):
        span = pl.ds(n * chunk, chunk)
        total = column_sum(z, span)
        for step in range(1, NZ):
            t_copies[n * (NZ - 1) + step - 1].wait_recv()
            total = total + r3[step - 1, :, span].astype(F32)
        grad_out[:, span] = total.astype(BF16)
    for copy in a_copies:
        copy.wait_recv()
    for copy in stores:
        copy.wait()
    sent = list(z_copies.values()) + y_copies + x_copies + d_copies + c_copies + u_copies[0]
    sent += u_copies[1] + v_copies + a_copies + p_copies + q_copies + t_copies
    for copy in sent:
        copy.wait_send()


def weight_panel(scale, kept_row, base, turned, dz, out, at):
    bs = dz.shape[-1]
    value = dz.reshape(-1, bs)
    for j in range(0, out.shape[1], 4):
        chosen = jnp.concatenate([turned[kept_row[base + j + t]] for t in range(4)], axis=0)
        grad = jnp.dot(chosen, value, preferred_element_type=F32) * scale
        out[at, j:j + 4] = grad.astype(BF16).reshape(4, bs, bs)


def finish_kernel(
    first, owner, act_in, grad_in, grads_in, act_out, grad_out, block_grad, grads, load, store
):
    slots = grads.shape[0]
    bs = act_in.shape[2]
    panels = act_out.shape[1] // bs
    loads = [
        pltpu.make_async_copy(grads_in.at[s], grads.at[s], load.at[s]) for s in range(slots)
    ]
    stores = [
        pltpu.make_async_copy(grads.at[s], block_grad.at[s], store.at[s]) for s in range(slots)
    ]
    for copy in loads:
        copy.start()
    for s in range(slots // 2):
        loads[s].wait()
        stores[s].start()
    grad_out[...] = grad_in[...]

    @pl.loop(0, panels)
    def _(c):
        k = owner[c]
        at = jnp.clip(k * slots + c - first[k], 0, NF * slots - 1)
        act_out[:, pl.ds(pl.multiple_of(c * bs, bs), bs)] = act_in[at]

    for s in range(slots // 2, slots):
        loads[s].wait()
        stores[s].start()
    for copy in stores:
        copy.wait()


def per_device(tokens, upstream, blocks, keep_mask, panel_owner):
    tok_dev, width = tokens.shape
    slots, keep, bs, _ = blocks.shape
    panels = panel_owner.shape[0]
    row_blocks = keep_mask.shape[0]
    reps = 2
    group = NF * tok_dev
    pairs = slots // 2
    shard_ids = jnp.arange(NF + 1, dtype=jnp.int32)
    below = (panel_owner[:, None] < shard_ids[None, :]).astype(jnp.int32)
    first = jnp.sum(below, axis=0)

    smem = pl.BlockSpec(memory_space=pltpu.SMEM)
    vmem = pl.BlockSpec(memory_space=pltpu.VMEM)
    anywhere = pl.BlockSpec(memory_space=pl.ANY)
    dma = lambda n: [pltpu.SemaphoreType.DMA((n,))] * 2
    scale = 1.0 / math.sqrt(group * reps)
    act_in, grad_in, grads = pl.pallas_call(
        functools.partial(layer_kernel, scale),
        out_shape=(
            jax.ShapeDtypeStruct((NF * slots, tok_dev, bs), BF16),
            jax.ShapeDtypeStruct((tok_dev, width), BF16),
            jax.ShapeDtypeStruct((slots, keep, bs, bs), BF16),
        ),
        in_specs=[smem, smem, vmem, vmem, anywhere],
        out_specs=(vmem, vmem, anywhere),
        scratch_shapes=[
            pltpu.VMEM((reps, NF, tok_dev, width), BF16),
            pltpu.VMEM((row_blocks, bs, reps * group), BF16),
            pltpu.VMEM((pairs, width, 2 * bs), BF16),
            pltpu.VMEM((slots * keep + 1, bs, bs), BF16),
            pltpu.VMEM((slots, keep, bs, bs), BF16),
            pltpu.VMEM((panels, tok_dev, bs), BF16),
            pltpu.VMEM((NF, slots, tok_dev, bs), BF16),
            pltpu.VMEM((NF, slots, tok_dev, bs), BF16),
            pltpu.VMEM((NF, slots, tok_dev, bs), BF16),
            pltpu.VMEM((slots, group, bs), F32),
            pltpu.VMEM((reps, slots, group, bs), BF16),
            pltpu.VMEM((pairs, group, 2 * bs), BF16),
            pltpu.VMEM((NZ, NY, NC, tok_dev, width), BF16),
            pltpu.VMEM((NZ, NY, tok_dev, width), BF16),
            pltpu.VMEM((NZ, tok_dev, width), BF16),
            pltpu.VMEM((NZ, tok_dev, width), BF16),
            pltpu.VMEM((NZ - 1, tok_dev, width), BF16),
            pltpu.VMEM((NZ - 1, tok_dev, width), BF16),
            pltpu.SMEM((slots * row_blocks,), jnp.int32),
            pltpu.SMEM((slots * row_blocks,), jnp.int32),
            pltpu.SMEM((slots * keep,), jnp.int32),
            pltpu.SemaphoreType.DMA((8,)),
        ]
        + dma(NZ - 1) + dma(NZ) + dma(NZ) + dma(NZ) + dma(4 * NZ) + dma(2 * (NF - 1))
        + dma(2) + dma(2 * (NF - 1)) + dma(4) + dma(4) + dma(4 * (NZ - 1)),
        compiler_params=pltpu.CompilerParams(
            collective_id=0, has_side_effects=True, vmem_limit_bytes=VMEM_LIMIT
        ),
        name="layer",
    )(first, keep_mask, tokens, upstream, blocks.reshape(slots * keep, bs, bs))
    act_out, input_grad, block_grad = pl.pallas_call(
        finish_kernel,
        out_shape=(
            jax.ShapeDtypeStruct((tok_dev, panels * bs), BF16),
            jax.ShapeDtypeStruct((tok_dev, width), BF16),
            jax.ShapeDtypeStruct((slots, keep, bs, bs), BF16),
        ),
        in_specs=[smem, smem, vmem, vmem, anywhere],
        out_specs=(vmem, vmem, anywhere),
        scratch_shapes=[
            pltpu.VMEM((slots, keep, bs, bs), BF16),
            pltpu.SemaphoreType.DMA((slots,)),
            pltpu.SemaphoreType.DMA((slots,)),
        ],
        compiler_params=pltpu.CompilerParams(vmem_limit_bytes=VMEM_LIMIT),
        name="finish",
    )(first, panel_owner, act_in, grad_in, grads)
    return (act_out, input_grad, block_grad)


def solution(mesh):
    fits = mesh.shape["rep"] == 2 and mesh.shape["fsdp"] == NF
    return jax.shard_map(
        per_device if fits else per_device_general,
        mesh=mesh,
        in_specs=(
            P(("rep", "fsdp"), None),
            P(("rep", "fsdp"), None),
            P("fsdp", None, None, None),
            P(),
            P(),
        ),
        out_specs=(P(("rep", "fsdp"), None), P(("rep", "fsdp"), None), P("fsdp", None, None, None)),
        check_vma=False,
    )
```

```python
import functools
import math

import jax
import jax.numpy as jnp
from jax import lax
from jax.experimental import pallas as pl
from jax.experimental.pallas import tpu as pltpu
from jax.sharding import PartitionSpec as P

BF16 = jnp.bfloat16
F32 = jnp.float32
MESH = pl.DeviceIdType.MESH
VMEM_LIMIT = 60 * 1024 * 1024
NZ, NY, NC = 4, 2, 2
NF = NZ * NY * NC


def per_device_general(tokens, upstream, blocks, keep_mask, panel_owner):
    shard_count = lax.axis_size("fsdp")
    own_index = lax.axis_index("fsdp")
    tok_dev = tokens.shape[0]
    model_width = tokens.shape[1]
    slot_count = blocks.shape[0]
    keep_count = blocks.shape[1]
    block_size = blocks.shape[3]
    row_blocks = keep_mask.shape[0]
    panel_count = panel_owner.shape[0]
    group_rows = tok_dev * shard_count
    rep_count = lax.axis_size("rep")
    shard_ids = jnp.arange(shard_count, dtype=jnp.int32)
    member = (panel_owner[:, None] == shard_ids[None, :]).astype(jnp.int32)
    counts = jnp.sum(member, axis=0)
    first_panel = jnp.cumsum(counts) - counts
    slot_ids = jnp.arange(slot_count, dtype=jnp.int32)
    panel_table = jnp.clip(first_panel[:, None] + slot_ids[None, :], 0, panel_count - 1)
    is_mine = shard_ids == own_index
    own_first = jnp.sum(jnp.where(is_mine, first_panel, 0))
    own_count = jnp.sum(jnp.where(is_mine, counts, 0))
    own_live = slot_ids < own_count
    own_panels = jnp.clip(own_first + slot_ids, 0, panel_count - 1)
    panel_ids = jnp.arange(panel_count, dtype=jnp.int32)
    panel_pick = (panel_ids[None, :] == own_panels[:, None]).astype(jnp.int32)
    running = jnp.cumsum(keep_mask, axis=0)
    own_running = jnp.sum(panel_pick[:, None, :] * running[None, :, :], axis=2)
    pick_ids = jnp.arange(keep_count, dtype=jnp.int32)
    own_rows = jnp.sum(
        (own_running[:, :, None] <= pick_ids[None, None, :]).astype(jnp.int32), axis=1
    )
    upstream_panels = jnp.transpose(upstream.reshape(tok_dev, panel_count, block_size), (1, 0, 2))
    outgoing = jnp.take(upstream_panels, panel_table.reshape(-1), axis=0)
    incoming = lax.all_to_all(outgoing, "fsdp", split_axis=0, concat_axis=1, tiled=True)
    group_tokens = lax.all_gather(tokens, "fsdp", axis=0, tiled=True)
    all_tokens = lax.all_gather(group_tokens, "rep", axis=0, tiled=True)
    token_blocks = jnp.transpose(all_tokens).reshape(row_blocks, block_size, rep_count * group_rows)

    dense_panels = jnp.zeros((slot_count, row_blocks, block_size, block_size), blocks.dtype)
    dense_panels = dense_panels.at[slot_ids[:, None], own_rows].set(blocks)
    dense = dense_panels.reshape(slot_count, model_width, block_size)
    preact = lax.dot_general(
        group_tokens, dense, (((1,), (1,)), ((), ())), preferred_element_type=jnp.float32
    )
    sigmoid_z = jax.nn.sigmoid(preact)
    activations = (preact * sigmoid_z).astype(jnp.bfloat16)
    slope = sigmoid_z * (1.0 + preact * (1.0 - sigmoid_z))
    cot = jnp.transpose(incoming, (1, 0, 2)).astype(jnp.float32)
    dpre = jnp.where(own_live[None, :, None], cot * slope, 0.0).astype(jnp.bfloat16)
    dpre_all = lax.all_gather(dpre, "rep", axis=0, tiled=True)
    backward = lax.dot_general(
        dpre, dense, (((1, 2), (0, 2)), ((), ())), preferred_element_type=jnp.float32
    )
    input_grad = lax.psum_scatter(
        backward, "fsdp", scatter_dimension=0, tiled=True
    ).astype(jnp.bfloat16)
    returned = lax.all_to_all(activations, "fsdp", split_axis=0, concat_axis=1, tiled=True)
    panel_first = jnp.sum(member * first_panel[None, :], axis=1)
    panel_slot = panel_owner * slot_count + panel_ids - panel_first
    act_panels = jnp.take(returned, panel_slot, axis=1)
    activation_out = act_panels.reshape(tok_dev, panel_count * block_size)
    scale = 1.0 / math.sqrt(group_rows * rep_count)

    def panel_step(nothing, item):
        row_ids, dz = item
        chosen = jnp.take(token_blocks, row_ids, axis=0)
        grad = lax.dot_general(
            chosen, dz, (((2,), (0,)), ((), ())), preferred_element_type=jnp.float32
        )
        return nothing, (grad * scale).astype(jnp.bfloat16)

    nothing, block_grad = lax.scan(
        panel_step, jnp.zeros((), jnp.float32), (own_rows, jnp.transpose(dpre_all, (1, 0, 2)))
    )
    return (activation_out, input_grad, block_grad)


class Place:
    def __init__(self):
        self.rep = lax.axis_index("rep")
        self.me = lax.axis_index("fsdp")
        self.core = self.me % NC
        self.y = (self.me // NC) % NY
        self.z = self.me // (NC * NY)

    def at(self, z, y, core):
        return (z * NY + y) * NC + core

    def z_back(self, step):
        return (self.z + NZ - step) % NZ

    def z_ahead(self, step):
        return (self.z + step) % NZ

    def fsdp_peer(self, step):
        return (self.me + step) % NF

    def greet(self):
        barrier = pltpu.get_barrier_semaphore()
        for step in range(1, NF):
            pl.semaphore_signal(
                barrier, inc=1, device_id=(self.rep, self.fsdp_peer(step)), device_id_type=MESH
            )
        pl.semaphore_signal(barrier, inc=1, device_id=(1 - self.rep, self.me), device_id_type=MESH)
        pl.semaphore_wait(barrier, NF)


def send(src, dst, sems, slot, device):
    send_sems, recv_sems = sems
    copy = pltpu.make_async_remote_copy(
        src_ref=src,
        dst_ref=dst,
        send_sem=send_sems.at[slot],
        recv_sem=recv_sems.at[slot],
        device_id=device,
        device_id_type=MESH,
    )
    copy.start()
    return copy


def layer_kernel(
    scale,
    first, keep, tokens, upstream, blocks_hbm,
    act_in, grad_out, grads_out,
    all_tokens, turned, dense, blocks, grads, up3, outgoing, incoming,
    act, slope, dz_both, dz_flat, part, r1, s2, r2, s3, r3, s4, r4, run, place_of, kept_row,
    local, z_s, z_r, y_s, y_r, x_s, x_r, d_s, d_r, c_s, c_r, u_s, u_r,
    v_s, v_r, a_s, a_r, p_s, p_r, q_s, q_r, t_s, t_r, w_s, w_r,
):
    place = Place()
    rep, me, z, y, core = place.rep, place.me, place.z, place.y, place.core
    slots, bs = outgoing.shape[1], outgoing.shape[3]
    row_blocks, panels = keep.shape
    kept = grads_out.shape[1]
    tok_dev, width = tokens.shape
    rows = NF * tok_dev
    pairs = slots // 2
    y_peer = (rep, place.at(z, 1 - y, core))
    x_peer = (1 - rep, me)
    core_peer = (rep, place.at(z, y, 1 - core))
    z_sems, y_sems, x_sems = (z_s, z_r), (y_s, y_r), (x_s, x_r)
    d_sems, c_sems, u_sems = (d_s, d_r), (c_s, c_r), (u_s, u_r)
    early = pairs // 2 + 1
    halves = ((0, 2 * early), (2 * early, slots - 2 * early))

    load_blocks = pltpu.make_async_copy(
        blocks_hbm, blocks.at[pl.ds(0, slots * kept)], local.at[0]
    )
    load_blocks.start()
    all_tokens[rep, me] = tokens[...]
    place.greet()

    far = (z + 2) % NZ
    near = z + 1 - 2 * (z % 2)
    line = (z, far, near, (near + 2) % NZ)
    far_peer = (rep, place.at(far, y, core))
    near_peer = (rep, place.at(near, y, core))
    own = all_tokens.at[rep, me]
    z_copies = [send(own, own, z_sems, 0, far_peer), send(own, own, z_sems, 1, near_peer)]
    y_copies, x_copies, d_copies, c_copies = [], [], [None] * NZ, [None] * (4 * NZ)

    def spread(step):
        piece = all_tokens.at[rep, place.at(line[step], y, core)]
        y_copies.append(send(piece, piece, y_sems, step, y_peer))
        x_copies.append(send(piece, piece, x_sems, step, x_peer))
        c_copies[step] = send(piece, piece, c_sems, step, core_peer)

    spread(0)

    for c in range(panels):
        up3[c] = upstream[:, c * bs:(c + 1) * bs]
    u_copies = [[], []]

    @pl.loop(0, NF)
    def _(k):
        for p in range(slots):
            outgoing[k, p] = up3[jnp.minimum(first[k] + p, panels - 1)]

    z_copies[0].wait_recv()
    piece = all_tokens.at[rep, place.at(far, y, core)]
    z_copies.append(send(piece, piece, z_sems, 2, near_peer))
    spread(1)
    z_copies[1].wait_recv()
    spread(2)
    for half, (start, size) in enumerate(halves):
        for step in range(1, NF):
            peer = place.fsdp_peer(step)
            span = pl.ds(start, size)
            u_copies[half].append(send(
                outgoing.at[peer, span], incoming.at[me, span], u_sems,
                half * (NF - 1) + step - 1, (rep, peer),
            ))
    incoming[me] = outgoing[me]

    @pl.loop(0, slots)
    def _(p):
        c = jnp.minimum(first[me] + p, panels - 1)
        count = jnp.int32(0)
        for r in range(row_blocks):
            bit = keep[r, c]
            count = count + bit
            run[p * row_blocks + r] = count
            place_of[p * row_blocks + r] = jnp.where(
                bit == 1, p * kept + jnp.clip(count - 1, 0, kept - 1), slots * kept
            )

    blocks[slots * kept] = jnp.zeros((bs, bs), BF16)
    load_blocks.wait()

    def build(start, stop):
        @pl.loop(start, stop)
        def _(i):
            for side in range(2):
                for r in range(row_blocks):
                    at = place_of[(2 * i + side) * row_blocks + r]
                    dense[i, r * bs:(r + 1) * bs, side * bs:(side + 1) * bs] = blocks[at]

    z_copies[2].wait_recv()
    spread(3)
    build(0, NZ - 1)
    for step in range(NZ):
        f_x = place.at(line[step], y, core)
        f_y = place.at(line[step], 1 - y, core)
        y_copies[step].wait_recv()
        piece = all_tokens.at[rep, f_y]
        c_copies[2 * NZ + step] = send(piece, piece, c_sems, 2 * NZ + step, core_peer)
        if step % 2 == 1:
            d_copies[step] = send(piece, piece, d_sems, step, x_peer)
        x_copies[step].wait_recv()
        piece = all_tokens.at[1 - rep, f_x]
        if step % 2 == 0:
            d_copies[step] = send(piece, piece, d_sems, step, y_peer)
        c_copies[NZ + step] = send(piece, piece, c_sems, NZ + step, core_peer)
        build(NZ - 1 + step, NZ + step)

    @pl.loop(0, slots)
    def _(p):
        @pl.loop(0, kept)
        def _(j):
            row = jnp.int32(0)
            for r in range(row_blocks):
                row = row + jnp.where(run[p * row_blocks + r] <= j, 1, 0)
            kept_row[p * kept + j] = jnp.minimum(row, row_blocks - 1)

    for step in range(NZ):
        c_copies[step].wait_recv()
        c_copies[2 * NZ + step].wait_recv()

    count = first[me + 1] - first[me]
    v_copies, a_copies = [], []
    for half, (start, size) in enumerate(halves):
        @pl.loop(start // 2, (start + size) // 2)
        def _(i):
            preact = jnp.dot(
                all_tokens[rep].reshape(rows, width), dense[i], preferred_element_type=F32
            )
            for side in range(2):
                slot = 2 * i + side
                zed = preact[:, side * bs:(side + 1) * bs]
                sig = jax.nn.sigmoid(zed)
                act[:, slot] = (zed * sig).astype(BF16).reshape(NF, tok_dev, bs)
                slope[slot] = sig * (1.0 + zed * (1.0 - sig))

        span = pl.ds(start, size)
        for step in range(1, NF):
            peer = place.fsdp_peer(step)
            a_copies.append(send(
                act.at[peer, span], act_in.at[pl.ds(me * slots + start, size)], (a_s, a_r),
                half * (NF - 1) + step - 1, (rep, peer),
            ))
        if half == 0:
            for step in range(NZ):
                d_copies[step].wait_recv()
                piece = all_tokens.at[1 - rep, place.at(line[step], 1 - y, core)]
                c_copies[3 * NZ + step] = send(piece, piece, c_sems, 3 * NZ + step, core_peer)
    act_in[pl.ds(me * slots, slots)] = act[me]

    def turn(group):
        @pl.loop(0, row_blocks)
        def _(r):
            lanes = pl.ds(pl.multiple_of(r * bs, bs), bs)
            span = pl.ds(pl.multiple_of(group * rows, rows), rows)
            turned[r, :, span] = all_tokens[group, :, :, lanes].reshape(rows, bs).T

    turn(rep)
    for half, (start, size) in enumerate(halves):
        for copy in u_copies[half]:
            copy.wait_recv()

        @pl.loop(start // 2, (start + size) // 2)
        def _(i):
            for side in range(2):
                slot = 2 * i + side
                cot = incoming[:, slot].reshape(rows, bs).astype(F32)
                value = jnp.where(slot < count, cot * slope[slot], 0.0).astype(BF16)
                dz_both[rep, slot] = value
                dz_flat[i, :, side * bs:(side + 1) * bs] = value

        piece = dz_both.at[rep, pl.ds(start, size)]
        v_copies.append(send(piece, piece, (v_s, v_r), half, x_peer))

    chunks = 4
    chunk = width // chunks
    p_copies, q_copies, t_copies, w_copies = [], [], [], []
    for n in range(chunks):
        span = pl.ds(n * chunk, chunk)
        total = jnp.zeros((rows, chunk), F32)
        for i in range(pairs):
            total = total + lax.dot_general(
                dz_flat[i], dense[i, span, :], (((1,), (1,)), ((), ())),
                preferred_element_type=F32,
            )
        part[:, :, :, :, span] = total.astype(BF16).reshape(NZ, NY, NC, tok_dev, chunk)
        p_copies.append(send(
            part.at[:, :, 1 - core, :, span], r1.at[:, :, :, span], (p_s, p_r), n, core_peer
        ))
    for n in range(chunks):
        span = pl.ds(n * chunk, chunk)
        p_copies[n].wait_recv()
        s2[:, :, span] = (
            part[:, 1 - y, core, :, span].astype(F32) + r1[:, 1 - y, :, span].astype(F32)
        ).astype(BF16)
        q_copies.append(send(s2.at[:, :, span], r2.at[:, :, span], (q_s, q_r), n, y_peer))

    def column_sum(at_z, span):
        return (
            part[at_z, y, core, :, span].astype(F32)
            + r1[at_z, y, :, span].astype(F32)
            + r2[at_z, :, span].astype(F32)
        )

    def to_near(n):
        span = pl.ds(n * chunk, chunk)
        q_copies[n].wait_recv()
        for t in range(2):
            s3[t, :, span] = column_sum(line[2 + t], span).astype(BF16)
        t_copies.append(send(s3.at[:, :, span], r3.at[:, :, span], (t_s, t_r), n, near_peer))

    def to_far(n):
        span = pl.ds(n * chunk, chunk)
        t_copies[n].wait_recv()
        s4[:, span] = (column_sum(far, span) + r3[1, :, span].astype(F32)).astype(BF16)
        w_copies.append(send(s4.at[:, span], r4.at[:, span], (w_s, w_r), n, far_peer))

    stores = []

    def store(src, dst):
        copy = pltpu.make_async_copy(src, dst, local.at[1 + len(stores)])
        copy.start()
        stores.append(copy)

    def weight(start, size):
        @pl.loop(start, start + size)
        def _(p):
            weight_panel(scale, kept_row, p * kept, turned, dz_both[:, p], grads, p)

        span = pl.ds(start, size)
        store(grads.at[span], grads_out.at[span])

    for step in range(NZ):
        c_copies[NZ + step].wait_recv()
        c_copies[3 * NZ + step].wait_recv()
    turn(1 - rep)
    for n in range(chunks):
        to_near(n)
    v_copies[0].wait_recv()
    cut = halves[0][1] // 2
    weight(0, cut)
    for n in range(chunks):
        to_far(n)
    weight(cut, halves[0][1] - cut)
    v_copies[1].wait_recv()
    weight(*halves[1])
    for n in range(chunks):
        span = pl.ds(n * chunk, chunk)
        w_copies[n].wait_recv()
        total = column_sum(z, span) + r3[0, :, span].astype(F32) + r4[:, span].astype(F32)
        grad_out[:, span] = total.astype(BF16)
    for copy in a_copies:
        copy.wait_recv()
    for copy in stores:
        copy.wait()
    sent = z_copies + y_copies + x_copies + d_copies + c_copies + u_copies[0]
    sent += u_copies[1] + v_copies + a_copies + p_copies + q_copies + t_copies + w_copies
    for copy in sent:
        copy.wait_send()


def weight_panel(scale, kept_row, base, turned, dz, out, at):
    bs = dz.shape[-1]
    value = dz.reshape(-1, bs)
    for j in range(0, out.shape[1], 4):
        chosen = jnp.concatenate([turned[kept_row[base + j + t]] for t in range(4)], axis=0)
        grad = jnp.dot(chosen, value, preferred_element_type=F32) * scale
        out[at, j:j + 4] = grad.astype(BF16).reshape(4, bs, bs)


def finish_kernel(
    first, owner, act_in, grad_in, grads_in, act_out, grad_out, block_grad, grads, load, store
):
    slots = grads.shape[0]
    bs = act_in.shape[2]
    panels = act_out.shape[1] // bs
    loads = [
        pltpu.make_async_copy(grads_in.at[s], grads.at[s], load.at[s]) for s in range(slots)
    ]
    stores = [
        pltpu.make_async_copy(grads.at[s], block_grad.at[s], store.at[s]) for s in range(slots)
    ]
    for copy in loads:
        copy.start()
    for s in range(slots // 2):
        loads[s].wait()
        stores[s].start()
    grad_out[...] = grad_in[...]

    @pl.loop(0, panels)
    def _(c):
        k = owner[c]
        at = jnp.clip(k * slots + c - first[k], 0, NF * slots - 1)
        act_out[:, pl.ds(pl.multiple_of(c * bs, bs), bs)] = act_in[at]

    for s in range(slots // 2, slots):
        loads[s].wait()
        stores[s].start()
    for copy in stores:
        copy.wait()


def per_device(tokens, upstream, blocks, keep_mask, panel_owner):
    tok_dev, width = tokens.shape
    slots, keep, bs, _ = blocks.shape
    panels = panel_owner.shape[0]
    row_blocks = keep_mask.shape[0]
    reps = 2
    group = NF * tok_dev
    pairs = slots // 2
    shard_ids = jnp.arange(NF + 1, dtype=jnp.int32)
    below = (panel_owner[:, None] < shard_ids[None, :]).astype(jnp.int32)
    first = jnp.sum(below, axis=0)

    smem = pl.BlockSpec(memory_space=pltpu.SMEM)
    vmem = pl.BlockSpec(memory_space=pltpu.VMEM)
    anywhere = pl.BlockSpec(memory_space=pl.ANY)
    dma = lambda n: [pltpu.SemaphoreType.DMA((n,))] * 2
    scale = 1.0 / math.sqrt(group * reps)
    act_in, grad_in, grads = pl.pallas_call(
        functools.partial(layer_kernel, scale),
        out_shape=(
            jax.ShapeDtypeStruct((NF * slots, tok_dev, bs), BF16),
            jax.ShapeDtypeStruct((tok_dev, width), BF16),
            jax.ShapeDtypeStruct((slots, keep, bs, bs), BF16),
        ),
        in_specs=[smem, smem, vmem, vmem, anywhere],
        out_specs=(vmem, vmem, anywhere),
        scratch_shapes=[
            pltpu.VMEM((reps, NF, tok_dev, width), BF16),
            pltpu.VMEM((row_blocks, bs, reps * group), BF16),
            pltpu.VMEM((pairs, width, 2 * bs), BF16),
            pltpu.VMEM((slots * keep + 1, bs, bs), BF16),
            pltpu.VMEM((slots, keep, bs, bs), BF16),
            pltpu.VMEM((panels, tok_dev, bs), BF16),
            pltpu.VMEM((NF, slots, tok_dev, bs), BF16),
            pltpu.VMEM((NF, slots, tok_dev, bs), BF16),
            pltpu.VMEM((NF, slots, tok_dev, bs), BF16),
            pltpu.VMEM((slots, group, bs), F32),
            pltpu.VMEM((reps, slots, group, bs), BF16),
            pltpu.VMEM((pairs, group, 2 * bs), BF16),
            pltpu.VMEM((NZ, NY, NC, tok_dev, width), BF16),
            pltpu.VMEM((NZ, NY, tok_dev, width), BF16),
            pltpu.VMEM((NZ, tok_dev, width), BF16),
            pltpu.VMEM((NZ, tok_dev, width), BF16),
            pltpu.VMEM((2, tok_dev, width), BF16),
            pltpu.VMEM((2, tok_dev, width), BF16),
            pltpu.VMEM((tok_dev, width), BF16),
            pltpu.VMEM((tok_dev, width), BF16),
            pltpu.SMEM((slots * row_blocks,), jnp.int32),
            pltpu.SMEM((slots * row_blocks,), jnp.int32),
            pltpu.SMEM((slots * keep,), jnp.int32),
            pltpu.SemaphoreType.DMA((8,)),
        ]
        + dma(NZ - 1) + dma(NZ) + dma(NZ) + dma(NZ) + dma(4 * NZ) + dma(2 * (NF - 1))
        + dma(2) + dma(2 * (NF - 1)) + dma(4) + dma(4) + dma(4) + dma(4),
        compiler_params=pltpu.CompilerParams(
            collective_id=0, has_side_effects=True, vmem_limit_bytes=VMEM_LIMIT
        ),
        name="layer",
    )(first, keep_mask, tokens, upstream, blocks.reshape(slots * keep, bs, bs))
    act_out, input_grad, block_grad = pl.pallas_call(
        finish_kernel,
        out_shape=(
            jax.ShapeDtypeStruct((tok_dev, panels * bs), BF16),
            jax.ShapeDtypeStruct((tok_dev, width), BF16),
            jax.ShapeDtypeStruct((slots, keep, bs, bs), BF16),
        ),
        in_specs=[smem, smem, vmem, vmem, anywhere],
        out_specs=(vmem, vmem, anywhere),
        scratch_shapes=[
            pltpu.VMEM((slots, keep, bs, bs), BF16),
            pltpu.SemaphoreType.DMA((slots,)),
            pltpu.SemaphoreType.DMA((slots,)),
        ],
        compiler_params=pltpu.CompilerParams(vmem_limit_bytes=VMEM_LIMIT),
        name="finish",
    )(first, panel_owner, act_in, grad_in, grads)
    return (act_out, input_grad, block_grad)


def solution(mesh):
    fits = mesh.shape["rep"] == 2 and mesh.shape["fsdp"] == NF
    return jax.shard_map(
        per_device if fits else per_device_general,
        mesh=mesh,
        in_specs=(
            P(("rep", "fsdp"), None),
            P(("rep", "fsdp"), None),
            P("fsdp", None, None, None),
            P(),
            P(),
        ),
        out_specs=(P(("rep", "fsdp"), None), P(("rep", "fsdp"), None), P("fsdp", None, None, None)),
        check_vma=False,
    )
```

```python
import functools
import math

import jax
import jax.numpy as jnp
from jax import lax
from jax.experimental import pallas as pl
from jax.experimental.pallas import tpu as pltpu
from jax.sharding import PartitionSpec as P

BF16 = jnp.bfloat16
F32 = jnp.float32
MESH = pl.DeviceIdType.MESH
VMEM_LIMIT = 60 * 1024 * 1024
NZ, NY, NC = 4, 2, 2
NF = NZ * NY * NC


def per_device_general(tokens, upstream, blocks, keep_mask, panel_owner):
    shard_count = lax.axis_size("fsdp")
    own_index = lax.axis_index("fsdp")
    tok_dev = tokens.shape[0]
    model_width = tokens.shape[1]
    slot_count = blocks.shape[0]
    keep_count = blocks.shape[1]
    block_size = blocks.shape[3]
    row_blocks = keep_mask.shape[0]
    panel_count = panel_owner.shape[0]
    group_rows = tok_dev * shard_count
    rep_count = lax.axis_size("rep")
    shard_ids = jnp.arange(shard_count, dtype=jnp.int32)
    member = (panel_owner[:, None] == shard_ids[None, :]).astype(jnp.int32)
    counts = jnp.sum(member, axis=0)
    first_panel = jnp.cumsum(counts) - counts
    slot_ids = jnp.arange(slot_count, dtype=jnp.int32)
    panel_table = jnp.clip(first_panel[:, None] + slot_ids[None, :], 0, panel_count - 1)
    is_mine = shard_ids == own_index
    own_first = jnp.sum(jnp.where(is_mine, first_panel, 0))
    own_count = jnp.sum(jnp.where(is_mine, counts, 0))
    own_live = slot_ids < own_count
    own_panels = jnp.clip(own_first + slot_ids, 0, panel_count - 1)
    panel_ids = jnp.arange(panel_count, dtype=jnp.int32)
    panel_pick = (panel_ids[None, :] == own_panels[:, None]).astype(jnp.int32)
    running = jnp.cumsum(keep_mask, axis=0)
    own_running = jnp.sum(panel_pick[:, None, :] * running[None, :, :], axis=2)
    pick_ids = jnp.arange(keep_count, dtype=jnp.int32)
    own_rows = jnp.sum(
        (own_running[:, :, None] <= pick_ids[None, None, :]).astype(jnp.int32), axis=1
    )
    upstream_panels = jnp.transpose(upstream.reshape(tok_dev, panel_count, block_size), (1, 0, 2))
    outgoing = jnp.take(upstream_panels, panel_table.reshape(-1), axis=0)
    incoming = lax.all_to_all(outgoing, "fsdp", split_axis=0, concat_axis=1, tiled=True)
    group_tokens = lax.all_gather(tokens, "fsdp", axis=0, tiled=True)
    all_tokens = lax.all_gather(group_tokens, "rep", axis=0, tiled=True)
    token_blocks = jnp.transpose(all_tokens).reshape(row_blocks, block_size, rep_count * group_rows)

    dense_panels = jnp.zeros((slot_count, row_blocks, block_size, block_size), blocks.dtype)
    dense_panels = dense_panels.at[slot_ids[:, None], own_rows].set(blocks)
    dense = dense_panels.reshape(slot_count, model_width, block_size)
    preact = lax.dot_general(
        group_tokens, dense, (((1,), (1,)), ((), ())), preferred_element_type=jnp.float32
    )
    sigmoid_z = jax.nn.sigmoid(preact)
    activations = (preact * sigmoid_z).astype(jnp.bfloat16)
    slope = sigmoid_z * (1.0 + preact * (1.0 - sigmoid_z))
    cot = jnp.transpose(incoming, (1, 0, 2)).astype(jnp.float32)
    dpre = jnp.where(own_live[None, :, None], cot * slope, 0.0).astype(jnp.bfloat16)
    dpre_all = lax.all_gather(dpre, "rep", axis=0, tiled=True)
    backward = lax.dot_general(
        dpre, dense, (((1, 2), (0, 2)), ((), ())), preferred_element_type=jnp.float32
    )
    input_grad = lax.psum_scatter(
        backward, "fsdp", scatter_dimension=0, tiled=True
    ).astype(jnp.bfloat16)
    returned = lax.all_to_all(activations, "fsdp", split_axis=0, concat_axis=1, tiled=True)
    panel_first = jnp.sum(member * first_panel[None, :], axis=1)
    panel_slot = panel_owner * slot_count + panel_ids - panel_first
    act_panels = jnp.take(returned, panel_slot, axis=1)
    activation_out = act_panels.reshape(tok_dev, panel_count * block_size)
    scale = 1.0 / math.sqrt(group_rows * rep_count)

    def panel_step(nothing, item):
        row_ids, dz = item
        chosen = jnp.take(token_blocks, row_ids, axis=0)
        grad = lax.dot_general(
            chosen, dz, (((2,), (0,)), ((), ())), preferred_element_type=jnp.float32
        )
        return nothing, (grad * scale).astype(jnp.bfloat16)

    nothing, block_grad = lax.scan(
        panel_step, jnp.zeros((), jnp.float32), (own_rows, jnp.transpose(dpre_all, (1, 0, 2)))
    )
    return (activation_out, input_grad, block_grad)


class Place:
    def __init__(self):
        self.rep = lax.axis_index("rep")
        self.me = lax.axis_index("fsdp")
        self.core = self.me % NC
        self.y = (self.me // NC) % NY
        self.z = self.me // (NC * NY)

    def at(self, z, y, core):
        return (z * NY + y) * NC + core

    def z_back(self, step):
        return (self.z + NZ - step) % NZ

    def z_ahead(self, step):
        return (self.z + step) % NZ

    def fsdp_peer(self, step):
        return (self.me + step) % NF

    def greet(self):
        barrier = pltpu.get_barrier_semaphore()
        for step in range(1, NF):
            pl.semaphore_signal(
                barrier, inc=1, device_id=(self.rep, self.fsdp_peer(step)), device_id_type=MESH
            )
        pl.semaphore_signal(barrier, inc=1, device_id=(1 - self.rep, self.me), device_id_type=MESH)
        pl.semaphore_wait(barrier, NF)


def send(src, dst, sems, slot, device):
    send_sems, recv_sems = sems
    copy = pltpu.make_async_remote_copy(
        src_ref=src,
        dst_ref=dst,
        send_sem=send_sems.at[slot],
        recv_sem=recv_sems.at[slot],
        device_id=device,
        device_id_type=MESH,
    )
    copy.start()
    return copy


def layer_kernel(
    scale,
    first, keep, tokens, upstream, blocks_hbm,
    act_in, grad_out, block_grad,
    all_tokens, turned, dense, blocks, grads, up3, outgoing, incoming,
    act, dz_both, dz_flat, part, r1, s2, r2, s3, r3, run, place_of, kept_row,
    local, z_s, z_r, y_s, y_r, x_s, x_r, d_s, d_r, c_s, c_r, u_s, u_r,
    v_s, v_r, a_s, a_r, p_s, p_r, q_s, q_r, t_s, t_r,
):
    place = Place()
    rep, me, z, y, core = place.rep, place.me, place.z, place.y, place.core
    slots, bs = outgoing.shape[1], outgoing.shape[3]
    row_blocks, panels = keep.shape
    kept = block_grad.shape[1]
    tok_dev, width = tokens.shape
    rows = NF * tok_dev
    pairs = slots // 2
    y_peer = (rep, place.at(z, 1 - y, core))
    x_peer = (1 - rep, me)
    core_peer = (rep, place.at(z, y, 1 - core))
    z_sems, y_sems, x_sems = (z_s, z_r), (y_s, y_r), (x_s, x_r)
    d_sems, c_sems, u_sems = (d_s, d_r), (c_s, c_r), (u_s, u_r)
    early = pairs // 2 + 1
    halves = ((0, 2 * early), (2 * early, slots - 2 * early))

    load_blocks = pltpu.make_async_copy(
        blocks_hbm, blocks.at[pl.ds(0, slots * kept)], local.at[0]
    )
    load_blocks.start()
    all_tokens[rep, me] = tokens[...]
    place.greet()

    own = all_tokens.at[rep, me]
    z_copies = {}
    for step in range(1, NZ):
        peer = (rep, place.at(place.z_ahead(step), y, core))
        z_copies[step] = send(own, own, z_sems, step - 1, peer)
    y_copies, x_copies, d_copies, c_copies = [], [], [None] * NZ, [None] * (4 * NZ)

    def spread(step):
        piece = all_tokens.at[rep, place.at(place.z_back(step), y, core)]
        y_copies.append(send(piece, piece, y_sems, step, y_peer))
        x_copies.append(send(piece, piece, x_sems, step, x_peer))
        c_copies[step] = send(piece, piece, c_sems, step, core_peer)

    spread(0)

    for c in range(panels):
        up3[c] = upstream[:, c * bs:(c + 1) * bs]
    u_copies = [[], []]
    for half, (start, size) in enumerate(halves):
        @pl.loop(0, NF)
        def _(k):
            for p in range(start, start + size):
                outgoing[k, p] = up3[jnp.minimum(first[k] + p, panels - 1)]

        for step in range(1, NF):
            peer = place.fsdp_peer(step)
            span = pl.ds(start, size)
            u_copies[half].append(send(
                outgoing.at[peer, span], incoming.at[me, span], u_sems,
                half * (NF - 1) + step - 1, (rep, peer),
            ))
    incoming[me] = outgoing[me]

    @pl.loop(0, slots)
    def _(p):
        c = jnp.minimum(first[me] + p, panels - 1)
        count = jnp.int32(0)
        for r in range(row_blocks):
            bit = keep[r, c]
            count = count + bit
            run[p * row_blocks + r] = count
            place_of[p * row_blocks + r] = jnp.where(
                bit == 1, p * kept + jnp.clip(count - 1, 0, kept - 1), slots * kept
            )

    blocks[slots * kept] = jnp.zeros((bs, bs), BF16)
    load_blocks.wait()

    def build(start, stop):
        @pl.loop(start, stop)
        def _(i):
            for side in range(2):
                for r in range(row_blocks):
                    at = place_of[(2 * i + side) * row_blocks + r]
                    dense[i, r * bs:(r + 1) * bs, side * bs:(side + 1) * bs] = blocks[at]

    for step in range(1, NZ):
        z_copies[step].wait_recv()
        spread(step)
        build(step - 1, step)
    for step in range(NZ):
        f_x = place.at(place.z_back(step), y, core)
        f_y = place.at(place.z_back(step), 1 - y, core)
        y_copies[step].wait_recv()
        piece = all_tokens.at[rep, f_y]
        c_copies[2 * NZ + step] = send(piece, piece, c_sems, 2 * NZ + step, core_peer)
        if step % 2 == 1:
            d_copies[step] = send(piece, piece, d_sems, step, x_peer)
        x_copies[step].wait_recv()
        piece = all_tokens.at[1 - rep, f_x]
        if step % 2 == 0:
            d_copies[step] = send(piece, piece, d_sems, step, y_peer)
        c_copies[NZ + step] = send(piece, piece, c_sems, NZ + step, core_peer)
        build(NZ - 1 + step, NZ + step)

    @pl.loop(0, slots)
    def _(p):
        @pl.loop(0, kept)
        def _(j):
            row = jnp.int32(0)
            for r in range(row_blocks):
                row = row + jnp.where(run[p * row_blocks + r] <= j, 1, 0)
            kept_row[p * kept + j] = jnp.minimum(row, row_blocks - 1)

    for step in range(NZ):
        c_copies[step].wait_recv()
        c_copies[2 * NZ + step].wait_recv()

    count = first[me + 1] - first[me]
    v_copies, a_copies = [], []
    for half, (start, size) in enumerate(halves):
        for copy in u_copies[half]:
            copy.wait_recv()

        @pl.loop(start // 2, (start + size) // 2)
        def _(i):
            preact = jnp.dot(
                all_tokens[rep].reshape(rows, width), dense[i], preferred_element_type=F32
            )
            for side in range(2):
                slot = 2 * i + side
                zed = preact[:, side * bs:(side + 1) * bs]
                sig = jax.nn.sigmoid(zed)
                act[:, slot] = (zed * sig).astype(BF16).reshape(NF, tok_dev, bs)
                slope = sig * (1.0 + zed * (1.0 - sig))
                cot = incoming[:, slot].reshape(rows, bs).astype(F32)
                value = jnp.where(slot < count, cot * slope, 0.0).astype(BF16)
                dz_both[rep, slot] = value
                dz_flat[i, :, side * bs:(side + 1) * bs] = value

        span = pl.ds(start, size)
        piece = dz_both.at[rep, span]
        v_copies.append(send(piece, piece, (v_s, v_r), half, x_peer))
        for step in range(1, NF):
            peer = place.fsdp_peer(step)
            a_copies.append(send(
                act.at[peer, span], act_in.at[pl.ds(me * slots + start, size)], (a_s, a_r),
                half * (NF - 1) + step - 1, (rep, peer),
            ))
        if half == 0:
            for step in range(NZ):
                d_copies[step].wait_recv()
                piece = all_tokens.at[1 - rep, place.at(place.z_back(step), 1 - y, core)]
                c_copies[3 * NZ + step] = send(piece, piece, c_sems, 3 * NZ + step, core_peer)
    act_in[pl.ds(me * slots, slots)] = act[me]

    chunks = 4
    chunk = width // chunks
    p_copies, q_copies, t_copies = [], [], []
    for n in range(chunks):
        span = pl.ds(n * chunk, chunk)
        total = jnp.zeros((rows, chunk), F32)
        for i in range(pairs):
            total = total + lax.dot_general(
                dz_flat[i], dense[i, span, :], (((1,), (1,)), ((), ())),
                preferred_element_type=F32,
            )
        part[:, :, :, :, span] = total.astype(BF16).reshape(NZ, NY, NC, tok_dev, chunk)
        p_copies.append(send(
            part.at[:, :, 1 - core, :, span], r1.at[:, :, :, span], (p_s, p_r), n, core_peer
        ))
    for n in range(chunks):
        span = pl.ds(n * chunk, chunk)
        p_copies[n].wait_recv()
        s2[:, :, span] = (
            part[:, 1 - y, core, :, span].astype(F32) + r1[:, 1 - y, :, span].astype(F32)
        ).astype(BF16)
        q_copies.append(send(s2.at[:, :, span], r2.at[:, :, span], (q_s, q_r), n, y_peer))

    def column_sum(at_z, span):
        return (
            part[at_z, y, core, :, span].astype(F32)
            + r1[at_z, y, :, span].astype(F32)
            + r2[at_z, :, span].astype(F32)
        )

    def to_z(n):
        span = pl.ds(n * chunk, chunk)
        q_copies[n].wait_recv()
        for step in range(1, NZ):
            s3[step - 1, :, span] = column_sum(place.z_ahead(step), span).astype(BF16)
            peer = (rep, place.at(place.z_ahead(step), y, core))
            t_copies.append(send(
                s3.at[step - 1, :, span], r3.at[step - 1, :, span], (t_s, t_r),
                n * (NZ - 1) + step - 1, peer,
            ))

    stores = []

    def weight(start, size):
        @pl.loop(start, start + size)
        def _(p):
            value = dz_both[:, p].reshape(2 * rows, bs)
            for j in range(kept):
                grads[p, j] = (
                    jnp.dot(
                        turned[kept_row[p * kept + j]], value, preferred_element_type=F32
                    ) * scale
                ).astype(BF16)

        span = pl.ds(start, size)
        stores.append(pltpu.make_async_copy(
            grads.at[span], block_grad.at[span], local.at[1 + len(stores)]
        ))
        stores[-1].start()

    for step in range(NZ):
        c_copies[NZ + step].wait_recv()
        c_copies[3 * NZ + step].wait_recv()

    @pl.loop(0, row_blocks)
    def _(r):
        lanes = pl.ds(pl.multiple_of(r * bs, bs), bs)
        turned[r] = all_tokens[:, :, :, lanes].reshape(2 * rows, bs).T

    v_copies[0].wait_recv()
    cut = halves[0][1] // 2
    to_z(0)
    weight(0, cut)
    to_z(1)
    to_z(2)
    weight(cut, halves[0][1] - cut)
    to_z(3)
    v_copies[1].wait_recv()
    weight(*halves[1])
    for n in range(chunks):
        span = pl.ds(n * chunk, chunk)
        total = column_sum(z, span)
        for step in range(1, NZ):
            t_copies[n * (NZ - 1) + step - 1].wait_recv()
            total = total + r3[step - 1, :, span].astype(F32)
        grad_out[:, span] = total.astype(BF16)
    for copy in a_copies:
        copy.wait_recv()

    for store in stores:
        store.wait()
    sent = list(z_copies.values()) + y_copies + x_copies + d_copies + c_copies + u_copies[0]
    sent += u_copies[1] + v_copies + a_copies + p_copies + q_copies + t_copies
    for copy in sent:
        copy.wait_send()


def finish_kernel(
    first, owner, act_in, grad_in, grads_in, act_out, grad_out, block_grad, grads, load, store
):
    slots = grads.shape[0]
    bs = act_in.shape[2]
    panels = act_out.shape[1] // bs
    loads = [
        pltpu.make_async_copy(grads_in.at[s], grads.at[s], load.at[s]) for s in range(slots)
    ]
    stores = [
        pltpu.make_async_copy(grads.at[s], block_grad.at[s], store.at[s]) for s in range(slots)
    ]
    for copy in loads:
        copy.start()
    for s in range(slots // 2):
        loads[s].wait()
        stores[s].start()
    grad_out[...] = grad_in[...]

    @pl.loop(0, panels)
    def _(c):
        k = owner[c]
        at = jnp.clip(k * slots + c - first[k], 0, NF * slots - 1)
        act_out[:, pl.ds(pl.multiple_of(c * bs, bs), bs)] = act_in[at]

    for s in range(slots // 2, slots):
        loads[s].wait()
        stores[s].start()
    for copy in stores:
        copy.wait()


def per_device(tokens, upstream, blocks, keep_mask, panel_owner):
    tok_dev, width = tokens.shape
    slots, keep, bs, _ = blocks.shape
    panels = panel_owner.shape[0]
    row_blocks = keep_mask.shape[0]
    reps = 2
    group = NF * tok_dev
    pairs = slots // 2
    shard_ids = jnp.arange(NF + 1, dtype=jnp.int32)
    below = (panel_owner[:, None] < shard_ids[None, :]).astype(jnp.int32)
    first = jnp.sum(below, axis=0)

    smem = pl.BlockSpec(memory_space=pltpu.SMEM)
    vmem = pl.BlockSpec(memory_space=pltpu.VMEM)
    anywhere = pl.BlockSpec(memory_space=pl.ANY)
    dma = lambda n: [pltpu.SemaphoreType.DMA((n,))] * 2
    act_in, grad_in, grads = pl.pallas_call(
        functools.partial(layer_kernel, 1.0 / math.sqrt(group * reps)),
        out_shape=(
            jax.ShapeDtypeStruct((NF * slots, tok_dev, bs), BF16),
            jax.ShapeDtypeStruct((tok_dev, width), BF16),
            jax.ShapeDtypeStruct((slots, keep, bs, bs), BF16),
        ),
        in_specs=[smem, smem, vmem, vmem, anywhere],
        out_specs=(vmem, vmem, anywhere),
        scratch_shapes=[
            pltpu.VMEM((reps, NF, tok_dev, width), BF16),
            pltpu.VMEM((row_blocks, bs, reps * group), BF16),
            pltpu.VMEM((pairs, width, 2 * bs), BF16),
            pltpu.VMEM((slots * keep + 1, bs, bs), BF16),
            pltpu.VMEM((slots, keep, bs, bs), BF16),
            pltpu.VMEM((panels, tok_dev, bs), BF16),
            pltpu.VMEM((NF, slots, tok_dev, bs), BF16),
            pltpu.VMEM((NF, slots, tok_dev, bs), BF16),
            pltpu.VMEM((NF, slots, tok_dev, bs), BF16),
            pltpu.VMEM((reps, slots, group, bs), BF16),
            pltpu.VMEM((pairs, group, 2 * bs), BF16),
            pltpu.VMEM((NZ, NY, NC, tok_dev, width), BF16),
            pltpu.VMEM((NZ, NY, tok_dev, width), BF16),
            pltpu.VMEM((NZ, tok_dev, width), BF16),
            pltpu.VMEM((NZ, tok_dev, width), BF16),
            pltpu.VMEM((NZ - 1, tok_dev, width), BF16),
            pltpu.VMEM((NZ - 1, tok_dev, width), BF16),
            pltpu.SMEM((slots * row_blocks,), jnp.int32),
            pltpu.SMEM((slots * row_blocks,), jnp.int32),
            pltpu.SMEM((slots * keep,), jnp.int32),
            pltpu.SemaphoreType.DMA((8,)),
        ]
        + dma(NZ - 1) + dma(NZ) + dma(NZ) + dma(NZ) + dma(4 * NZ) + dma(2 * (NF - 1))
        + dma(2) + dma(2 * (NF - 1)) + dma(4) + dma(4) + dma(4 * (NZ - 1)),
        compiler_params=pltpu.CompilerParams(
            collective_id=0, has_side_effects=True, vmem_limit_bytes=VMEM_LIMIT
        ),
        name="layer",
    )(first, keep_mask, tokens, upstream, blocks.reshape(slots * keep, bs, bs))
    act_out, input_grad, block_grad = pl.pallas_call(
        finish_kernel,
        out_shape=(
            jax.ShapeDtypeStruct((tok_dev, panels * bs), BF16),
            jax.ShapeDtypeStruct((tok_dev, width), BF16),
            jax.ShapeDtypeStruct((slots, keep, bs, bs), BF16),
        ),
        in_specs=[smem, smem, vmem, vmem, anywhere],
        out_specs=(vmem, vmem, anywhere),
        scratch_shapes=[
            pltpu.VMEM((slots, keep, bs, bs), BF16),
            pltpu.SemaphoreType.DMA((slots,)),
            pltpu.SemaphoreType.DMA((slots,)),
        ],
        compiler_params=pltpu.CompilerParams(vmem_limit_bytes=VMEM_LIMIT),
        name="finish",
    )(first, panel_owner, act_in, grad_in, grads)
    return (act_out, input_grad, block_grad)


def solution(mesh):
    fits = mesh.shape["rep"] == 2 and mesh.shape["fsdp"] == NF
    return jax.shard_map(
        per_device if fits else per_device_general,
        mesh=mesh,
        in_specs=(
            P(("rep", "fsdp"), None),
            P(("rep", "fsdp"), None),
            P("fsdp", None, None, None),
            P(),
            P(),
        ),
        out_specs=(P(("rep", "fsdp"), None), P(("rep", "fsdp"), None), P("fsdp", None, None, None)),
        check_vma=False,
    )
```
